32 devices in a mesh: row: 4 (over y, x), col: 8 (over z, core).
Axes of the slice: x: 2, y: 2, z: 4, core: 2. Of those that a mesh axis runs over, the one named last changes fastest.
Arguments:
- source: float32 [256, 64, 128], P(('row', 'col')), may hold values from -6 to 6
- blocks: float32 [8192, 64, 64], P(('row', 'col')), may hold values from -0.15625 to 0.15625
- row_index: int32 [8192], P(('row', 'col')), may hold values from 0 to 63
- col_index: int32 [8192], P(('row', 'col')), may hold values from 0 to 31
- live_count: int32 [32], P(('row', 'col')), may hold values from 64 to 256, as said below
Outputs:
- irradiance: float32 [256, 64, 128], P(('row', 'col'))
The draws below stay inside these ranges and needn't reach their ends.
Inputs may be any that keep to these rules, and one draw needn't show every extreme that they name: `live_count`: slots of a device beyond its live count are padding; some device has all 256 slots live.
All inputs are finite; a program needn't handle non-finite values.
Results may differ from the reference program's by a relative error of at most 0.0003.
Values sent between devices are 32-bit elements; how exact they have to be, the bound alone decides.
No kernel may reach another device: no remote copies, remote signals or barrier semaphores. Data moves between devices by JAX's collectives and lax.ppermute only.
A program may use at most 128 MiB of HBM per device.

```python
import jax
import jax.numpy as jnp
from jax import lax

BLOCK = 64
LIGHTS = 128
SLOTS = 32
ITERS = 2
BR_DEV = 8
NNZ_DEV = 256
BRICKS = 256
N_ROW = 4
N_COL = 8


def draw_live_count(key, part):
    counts = jax.random.randint(key, (N_ROW * N_COL,), NNZ_DEV // 4, NNZ_DEV + 1)
    chosen = jax.random.randint(jax.random.fold_in(key, 7), (), 0, N_ROW * N_COL)
    return counts.at[chosen].set(NNZ_DEV).astype(jnp.int32)


def place_ends(array, rng, smallest, largest):
    longest = array.shape.index(max(array.shape))
    spots = []
    for shift in (0, 1):
        where = [jax.random.randint(jax.random.fold_in(rng, axis), (), 0, length) for axis, length in enumerate(array.shape)]
        where[longest] = (where[longest] + shift) % array.shape[longest]
        spots.append(tuple(where))
    return array.at[spots[0]].set(smallest).at[spots[1]].set(largest)


def levels(key, shape, shards, low, high):
    def one(axis_at, blocks):
        draws = jax.random.uniform(jax.random.fold_in(jax.random.fold_in(key, 6), axis_at), (blocks,), jnp.float32, low / len(shards), high / len(shards))
        return jnp.repeat(jnp.exp(draws), shape[axis_at] // blocks).reshape((-1,) + (1,) * (len(shape) - axis_at - 1))

    factor_of = one(*shards[0])
    for cut in shards[1:]:
        factor_of = factor_of * one(*cut)
    return factor_of


def normal_values(key, extent, deviation, limit, split=(), kind=jnp.bfloat16):
    values = deviation * jax.random.normal(key, extent, jnp.float32)
    if split:
        values = values * levels(key, extent, split, -0.22, 0.18)
    return jnp.clip(values, -limit, limit).astype(kind)


def setup_inputs(seed: int = 0) -> dict:
    streams_of = jax.random.split(jax.random.key(seed), 6)
    return {
        "source": normal_values(streams_of[0], (BRICKS, BLOCK, LIGHTS), 1.0, 6.0, ((0, 32),), jnp.float32),
        "blocks": normal_values(streams_of[1], (BRICKS * SLOTS, BLOCK, BLOCK), (BLOCK * 20) ** -0.5, 0.15625, ((0, 32),), jnp.float32),
        "row_index": place_ends(jax.random.randint(streams_of[2], (BRICKS * SLOTS,), 0, BR_DEV * N_COL), jax.random.fold_in(streams_of[2], 1), 0, (BR_DEV * N_COL) - 1).astype(jnp.int32),
        "col_index": place_ends(jax.random.randint(streams_of[3], (BRICKS * SLOTS,), 0, BR_DEV * N_ROW), jax.random.fold_in(streams_of[3], 1), 0, (BR_DEV * N_ROW) - 1).astype(jnp.int32),
        "live_count": draw_live_count(jax.random.fold_in(streams_of[5], 71), 0),
    }


def transfer(field, blocks, row_index, col_index, live_count):
    group_rows = BR_DEV * N_COL
    slot_ids = jnp.arange(NNZ_DEV, dtype=jnp.int32)

    def row_group(r):
        def over_col(running, c):
            device = (r * N_COL + c).astype(jnp.int32)
            first = (device * NNZ_DEV).astype(jnp.int32)
            block_set = lax.dynamic_slice_in_dim(blocks, first, NNZ_DEV, 0)
            rows_here = lax.dynamic_slice_in_dim(row_index, first, NNZ_DEV, 0)
            cols_here = lax.dynamic_slice_in_dim(col_index, first, NNZ_DEV, 0)
            live_mask = slot_ids < live_count[device]
            global_col = (((cols_here // BR_DEV) * N_COL + c) * BR_DEV + cols_here % BR_DEV).astype(jnp.int32)
            picked = jnp.take(field, global_col, axis=0)
            products = jnp.einsum("nij,njl->nil", block_set, picked, precision=lax.Precision.HIGHEST)
            products = jnp.where(live_mask[:, None, None], products, jnp.zeros_like(products))
            return running + jax.ops.segment_sum(products, rows_here, num_segments=group_rows), None

        start = jnp.zeros((group_rows, field.shape[1], field.shape[2]), jnp.float32)
        result, _ = lax.scan(over_col, start, jnp.arange(N_COL, dtype=jnp.int32))
        return result

    stacked = lax.map(row_group, jnp.arange(N_ROW, dtype=jnp.int32))
    return stacked.reshape(field.shape)


def reference(source, blocks, row_index, col_index, live_count):
    field = source
    for bounce in range(ITERS):
        field = source + transfer(field, blocks, row_index, col_index, live_count)
    return field
```

```python
import functools

import jax
import jax.numpy as jnp
from jax import lax
from jax.experimental import pallas as pl
from jax.experimental.pallas import tpu as pltpu
from jax.sharding import PartitionSpec as P

ITERS = 2
HALVES = 2
GROUP = 32
BF16 = jnp.bfloat16
F32 = jnp.float32


def split_parts(value):
    high = value.astype(BF16)
    low = (value - high.astype(F32)).astype(BF16)
    return high, low


def prepare_kernel(b_ref, o_ref, t_ref):
    cells, _, slots = b_ref.shape
    width = min(128, slots)

    def turn(i, carry):
        for c in range(slots // width):
            value = b_ref[i, :, pl.ds(c * width, width)]
            high = value.astype(BF16).astype(F32)
            t_ref[i, pl.ds(c * width, width), :] = jnp.concatenate([high, value - high], axis=0).T
        return carry

    lax.fori_loop(0, cells, turn, 0, unroll=4)

    def regroup(g, carry):
        first = pl.multiple_of(g * 8, 8)
        o_ref[pl.ds(first, 8)] = jnp.swapaxes(t_ref[:, pl.ds(first, 8), :], 0, 1).astype(BF16)
        return carry

    lax.fori_loop(0, slots // 8, regroup, 0)


def prepare(blocks):
    slots, cells, _ = blocks.shape
    whole = pl.BlockSpec(memory_space=pltpu.VMEM)
    return pl.pallas_call(
        prepare_kernel,
        in_specs=[whole],
        out_specs=whole,
        out_shape=jax.ShapeDtypeStruct((slots, cells, 2 * cells), BF16),
        scratch_shapes=[pltpu.VMEM((cells, slots, 2 * cells), F32)],
        compiler_params=pltpu.CompilerParams(vmem_limit_bytes=32 * 2**20),
        cost_estimate=pl.CostEstimate(flops=0, bytes_accessed=24 * 2**20, transcendentals=0),
        name="prepare",
    )(jnp.transpose(blocks, (1, 2, 0)))


def transfer_kernel(n_in, n_out, place_ref, sender_ref, live_ref, a_ref, *rest):
    x_refs, out_refs = rest[:n_in], rest[n_in : n_in + n_out]
    w_ref, acc_ref, sems = rest[n_in + n_out :]
    base = 0
    for x_ref in x_refs:

        def split_brick(c, carry, x_ref=x_ref, base=base):
            w_ref[base + c] = jnp.concatenate(split_parts(x_ref[c]), axis=0)
            return carry

        lax.fori_loop(0, x_ref.shape[0], split_brick, 0, unroll=4)
        base += x_ref.shape[0]

    def clear(c, carry):
        acc_ref[c] = jnp.zeros(acc_ref.shape[1:], F32)
        return carry

    lax.fori_loop(0, acc_ref.shape[0], clear, 0, unroll=5)
    cells = acc_ref.shape[1]

    def step(g, carry):
        results = []
        for u in range(GROUP):
            s = g * GROUP + u
            a = a_ref[s]
            w = w_ref[sender_ref[s]]
            high, low = w[:cells], w[cells:]
            results.append(
                jnp.dot(
                    jnp.concatenate([a, a], axis=1),
                    jnp.concatenate([high, high, low, low], axis=0),
                    preferred_element_type=F32,
                )
            )
        for u in range(GROUP):
            acc_ref[place_ref[g * GROUP + u]] += results[u]
        return carry

    lax.fori_loop(0, (live_ref[0] + GROUP - 1) // GROUP, step, 0)
    copies, base = [], 0
    for i, out_ref in enumerate(out_refs):
        copies.append(pltpu.make_async_copy(acc_ref.at[pl.ds(base, out_ref.shape[0])], out_ref, sems.at[i]))
        base += out_ref.shape[0]
    for copy in copies:
        copy.start()
    for copy in copies:
        copy.wait()


def transfer(place, sender, live, matrix, fields, out_bricks):
    cells, lights = fields[0].shape[1:]
    bricks = sum(f.shape[0] for f in fields)
    whole = pl.BlockSpec(memory_space=pltpu.VMEM)
    scalars = pl.BlockSpec(memory_space=pltpu.SMEM)
    rows = matrix.shape[0] * cells
    return pl.pallas_call(
        functools.partial(transfer_kernel, len(fields), len(out_bricks)),
        in_specs=[scalars] * 3 + [whole] * (1 + len(fields)),
        out_specs=[pl.BlockSpec(memory_space=pl.ANY)] * len(out_bricks),
        out_shape=[jax.ShapeDtypeStruct((n, cells, lights), F32) for n in out_bricks],
        scratch_shapes=[
            pltpu.VMEM((bricks, 2 * cells, lights), BF16),
            pltpu.VMEM((sum(out_bricks) + 1, cells, lights), F32),
            pltpu.SemaphoreType.DMA((len(out_bricks),)),
        ],
        compiler_params=pltpu.CompilerParams(vmem_limit_bytes=32 * 2**20),
        cost_estimate=pl.CostEstimate(flops=2 * rows * 4 * cells * lights, bytes_accessed=16 * 2**20, transcendentals=0),
        name="transfer",
    )(place, sender, live, matrix, *fields)


def places(row_index, live, bricks, n_col):
    pairs, half = n_col // 2, bricks // HALVES
    me = lax.axis_index("col")
    my_pair, my_side = me // 2, me % 2
    column, brick = row_index // bricks, row_index % bricks
    pair, side = column // 2, column % 2
    ahead = jnp.where(my_side == 0, pair - my_pair, my_pair - pair) % pairs
    carrier = jnp.where(pair > my_pair, 0, jnp.where(pair < my_pair, 1, my_side))
    within = (ahead * 2 + (side ^ carrier)) * half + brick % half
    place = (brick // half) * (pairs * 2 * half) + within
    slots = jnp.arange(row_index.shape[0], dtype=jnp.int32)
    return jnp.where(slots < live, place, bricks * n_col).astype(jnp.int32)


def body(source, blocks, row_index, col_index, live_count):
    bricks = source.shape[0]
    n_row, n_col = lax.axis_size("row"), lax.axis_size("col")
    pairs, half = n_col // 2, bricks // HALVES
    my_row, my_col = lax.axis_index("row"), lax.axis_index("col")
    live = live_count[0]

    swap = [(i, i ^ 1) for i in range(n_col)]
    ring = [(i, (i + 2 if i + 2 < n_col else n_col - 1) if i % 2 == 0 else (i - 2 if i > 2 else 0)) for i in range(n_col)]
    first_of_line = jnp.where(my_col % 2 == 0, my_col == 0, my_col == n_col - 1)

    place = places(row_index, live, bricks, n_col)
    from_row = col_index // bricks
    flips = n_row & (n_row - 1) == 0
    turn = from_row ^ my_row if flips else (from_row - my_row) % n_row
    sender = (turn * bricks + col_index % bricks).astype(jnp.int32)
    matrix = prepare(blocks)

    def gather(value):
        fields = [value]
        for k in range(1, n_row):
            fields.append(lax.ppermute(value, "row", [(i ^ k if flips else (i + k) % n_row, i) for i in range(n_row)]))
        return fields

    def scatter(own, sent):
        got = lax.ppermute(sent, "col", swap)
        block = 2 * half

        def both(distance):
            mine, other = half + (distance - 1) * block, half + (pairs - distance - 1) * block
            return sent[mine : mine + block] + got[other : other + block]

        total = both(pairs - 1) if pairs > 1 else None
        for distance in range(pairs - 1, 0, -1):
            came = jnp.where(first_of_line, 0.0, lax.ppermute(total, "col", ring))
            total = came if distance == 1 else came + both(distance - 1)
        out = own + got[:half]
        if total is not None:
            out = out + total[:half] + lax.ppermute(total[half:], "col", swap)
        return out

    field = source
    sizes = [half, (2 * pairs - 1) * half] * HALVES
    for bounce in range(ITERS):
        sums = transfer(place, sender, live_count, matrix, gather(field), sizes)
        parts = [scatter(sums[2 * h], sums[2 * h + 1]) for h in range(HALVES)]
        field = source + jnp.concatenate(parts, axis=0)
    return field


def solution(mesh):
    in_specs = (
        P(("row", "col"), None, None),
        P(("row", "col"), None, None),
        P(("row", "col")),
        P(("row", "col")),
        P(("row", "col")),
    )
    out_specs = P(("row", "col"), None, None)
    return jax.shard_map(body, mesh=mesh, in_specs=in_specs, out_specs=out_specs, check_vma=False)
```

```python
import functools

import jax
import jax.numpy as jnp
from jax import lax
from jax.experimental import pallas as pl
from jax.experimental.pallas import tpu as pltpu
from jax.sharding import PartitionSpec as P

ITERS = 2
HALVES = 2
GROUP = 32
CHUNK = 16
PLAN_HEAD = 8
MIB = 2**20
SMALL = 2 * MIB
BF16 = jnp.bfloat16
F32 = jnp.float32


def split_parts(value):
    high = value.astype(BF16)
    low = (value - high.astype(F32)).astype(BF16)
    return high, low


def prepare_kernel(b_hbm, o_ref, b_ref, t_ref, sems):
    cells, _, slots = b_hbm.shape
    width = min(128, slots)
    rounds = cells // CHUNK
    copies = [
        pltpu.make_async_copy(b_hbm.at[pl.ds(r * CHUNK, CHUNK)], b_ref.at[pl.ds(r * CHUNK, CHUNK)], sems.at[r])
        for r in range(rounds)
    ]
    for copy in copies:
        copy.start()
    o_ref[slots] = jnp.zeros(o_ref.shape[1:], BF16)
    for r in range(rounds):
        copies[r].wait()

        def turn(i, carry, r=r):
            for c in range(slots // width):
                value = b_ref[r * CHUNK + i, :, pl.ds(c * width, width)]
                high = value.astype(BF16).astype(F32)
                t_ref[i, pl.ds(c * width, width), :] = jnp.concatenate([high, value - high], axis=0).T
            return carry

        lax.fori_loop(0, CHUNK, turn, 0, unroll=4)

        def regroup(g, carry, r=r):
            first = pl.multiple_of(g * 8, 8)
            o_ref[pl.ds(first, 8), pl.ds(r * CHUNK, CHUNK), :] = jnp.swapaxes(t_ref[:, pl.ds(first, 8), :], 0, 1).astype(BF16)
            return carry

        lax.fori_loop(0, slots // 8, regroup, 0, unroll=2)


def prepare(blocks):
    slots, cells, _ = blocks.shape
    return pl.pallas_call(
        prepare_kernel,
        in_specs=[pl.BlockSpec(memory_space=pltpu.HBM)],
        out_specs=pl.BlockSpec(memory_space=pltpu.VMEM),
        out_shape=jax.ShapeDtypeStruct((slots + 1, cells, 2 * cells), BF16),
        scratch_shapes=[
            pltpu.VMEM((cells, cells, slots), F32),
            pltpu.VMEM((CHUNK, slots, 2 * cells), F32),
            pltpu.SemaphoreType.DMA((cells // CHUNK,)),
        ],
        compiler_params=pltpu.CompilerParams(vmem_limit_bytes=14 * MIB),
        cost_estimate=pl.CostEstimate(flops=0, bytes_accessed=24 * MIB, transcendentals=0),
        name="prepare",
    )(pltpu.with_memory_space_constraint(jnp.transpose(blocks, (1, 2, 0)), pltpu.HBM))


def transfer_kernel(fields_at, jobs, n_before, plan_ref, a_ref, *rest):
    x_refs, rest = rest[: len(fields_at)], rest[len(fields_at) :]
    before_refs, out_refs, w_ref = rest[:n_before], rest[-1 - len(jobs) : -1], rest[-1]
    zero_slot, cells = a_ref.shape[0] - 1, a_ref.shape[1]
    length = (plan_ref.shape[0] - PLAN_HEAD) // 3
    for x_ref, at in zip(x_refs, fields_at):

        def split_brick(c, carry, x_ref=x_ref, at=at):
            w_ref[at + c] = jnp.concatenate(split_parts(x_ref[c]), axis=0)
            return carry

        lax.fori_loop(0, x_ref.shape[0], split_brick, 0, unroll=True)

    for n, ((begin, end), out_ref) in enumerate(zip(jobs, out_refs)):

        def clear(c, carry, n=n, out_ref=out_ref):
            out_ref[c] = before_refs[n][c] if n_before else jnp.zeros(out_ref.shape[1:], F32)
            return carry

        lax.fori_loop(0, out_ref.shape[0], clear, 0, unroll=4)
        first, last = plan_ref[begin], plan_ref[end]

        def step(g, carry, first=first, last=last, out_ref=out_ref):
            results, targets = [], []
            for u in range(GROUP):
                s = first + g * GROUP + u
                inside = s < last
                a = a_ref[jnp.where(inside, plan_ref[PLAN_HEAD + s], zero_slot)]
                w = w_ref[plan_ref[PLAN_HEAD + 2 * length + s]]
                targets.append(plan_ref[PLAN_HEAD + length + s])
                high, low = w[:cells], w[cells:]
                results.append(
                    jnp.dot(
                        jnp.concatenate([a, a], axis=1),
                        jnp.concatenate([high, high, low, low], axis=0),
                        preferred_element_type=F32,
                    )
                )
            for u in range(GROUP):
                out_ref[targets[u]] += results[u]
            return carry

        lax.fori_loop(0, (last - first + GROUP - 1) // GROUP, step, 0)


def transfer(plan, matrix, fields, fields_at, senders, jobs, before, out_bricks):
    cells, lights = fields[0].shape[1:]
    whole = pl.BlockSpec(memory_space=pltpu.VMEM)
    scratch = senders * 2 * cells * lights * 2
    rows = matrix.shape[0] * cells * sum(end - begin for begin, end in jobs) // HALVES**2
    return pl.pallas_call(
        functools.partial(transfer_kernel, fields_at, jobs, len(before)),
        in_specs=[pl.BlockSpec(memory_space=pltpu.SMEM)] + [whole] * (1 + len(fields) + len(before)),
        out_specs=[whole] * len(jobs),
        out_shape=[jax.ShapeDtypeStruct((out_bricks, cells, lights), F32)] * len(jobs),
        scratch_shapes=[pltpu.VMEM((senders, 2 * cells, lights), BF16)],
        compiler_params=pltpu.CompilerParams(vmem_limit_bytes=SMALL + scratch),
        cost_estimate=pl.CostEstimate(flops=2 * rows * 4 * cells * lights, bytes_accessed=8 * MIB, transcendentals=0),
        name="transfer",
    )(plan, matrix, *fields, *before)


def first_of_line():
    me, n = lax.axis_index("col"), lax.axis_size("col")
    return jnp.where(me % 2 == 0, me == 0, me == n - 1)


def small_call(kernel, out_bricks, name, *args, after=()):
    whole, anywhere = pl.BlockSpec(memory_space=pltpu.VMEM), pl.BlockSpec(memory_space=pl.ANY)
    shape = args[0].shape[1:]
    return pl.pallas_call(
        kernel,
        in_specs=[whole] * len(args) + [anywhere] * len(after),
        out_specs=[whole] * len(out_bricks),
        out_shape=[jax.ShapeDtypeStruct((n, *shape), F32) for n in out_bricks],
        compiler_params=pltpu.CompilerParams(vmem_limit_bytes=SMALL),
        cost_estimate=pl.CostEstimate(flops=0, bytes_accessed=MIB, transcendentals=0),
        name=name,
    )(*args, *after)


def block_of(distance):
    return {0: 1, 1: 0}.get(distance, distance)


def carry_kernel(mine, other, sums_ref, got_ref, *rest):
    came_refs, out_ref = rest[:-1], rest[-1]
    first = first_of_line()
    for c in range(out_ref.shape[0]):
        total = sums_ref[mine + c] + got_ref[other + c]
        if came_refs:
            total += jnp.where(first, 0.0, came_refs[0][c])
        out_ref[c] = total


def finish_kernel(n_halves, half_at, own, source_ref, *rest):
    out_ref = rest[-1]
    first = first_of_line()
    per = (len(rest) - 1) // n_halves
    for h in range(n_halves):
        sums_ref, got_ref, *ends = rest[h * per : (h + 1) * per]
        half = out_ref.shape[0] // n_halves
        for c in range(half):
            total = source_ref[(half_at + h) * half + c] + (sums_ref[own + c] + got_ref[half + c])
            if ends:
                total += jnp.where(first, 0.0, ends[0][c]) + ends[1][c]
            out_ref[h * half + c] = total


def cross_kernel(n_after, came_ref, *rest):
    out_ref = rest[n_after]
    half = out_ref.shape[0]
    first = first_of_line()
    for c in range(half):
        out_ref[c] = jnp.where(first, 0.0, came_ref[half + c])


def tail_kernel(value_ref, _, out_ref):
    out_ref[...] = value_ref[value_ref.shape[0] - out_ref.shape[0] :]


def make_plan(row_index, col_index, live, bricks, n_row, n_col, flips):
    pairs, half = n_col // 2, bricks // HALVES
    my_row, me = lax.axis_index("row"), lax.axis_index("col")
    my_pair, my_side = me // 2, me % 2
    column, brick = row_index // bricks, row_index % bricks
    pair, side = column // 2, column % 2
    ahead = jnp.where(my_side == 0, pair - my_pair, my_pair - pair) % pairs
    ahead = jnp.where(ahead < 2, 1 - ahead, ahead) if pairs > 1 else ahead
    carrier = jnp.where(pair > my_pair, 0, jnp.where(pair < my_pair, 1, my_side))
    place = (ahead * 2 + (side ^ carrier)) * half + brick % half

    from_row, from_brick = col_index // bricks, col_index % bricks
    turn = from_row ^ my_row if flips else (from_row - my_row) % n_row
    sender = turn * bricks + from_brick

    n = row_index.shape[0]
    slots = jnp.arange(n, dtype=jnp.int32)
    part = (brick // half) * HALVES + from_brick // half
    part = jnp.where(slots < live, part, HALVES**2)
    key = part * n + slots
    rank = jnp.sum(key[None, :] < key[:, None], axis=1, dtype=jnp.int32)
    chosen = rank[None, :] == jnp.arange(n + GROUP, dtype=jnp.int32)[:, None]

    def in_order(value):
        return jnp.sum(jnp.where(chosen, value[None, :], 0), axis=1, dtype=jnp.int32)

    bounds = jnp.arange(PLAN_HEAD, dtype=jnp.int32)
    starts = jnp.sum(part[None, :] < bounds[:, None], axis=1, dtype=jnp.int32)
    return jnp.concatenate([starts, in_order(slots), in_order(place), in_order(sender)])


def body(source, blocks, row_index, col_index, live_count):
    bricks = source.shape[0]
    n_row, n_col = lax.axis_size("row"), lax.axis_size("col")
    pairs, half = n_col // 2, bricks // HALVES
    block = 2 * half
    flips = n_row & (n_row - 1) == 0

    swap = [(i, i ^ 1) for i in range(n_col)]
    ring = [(i, (i + 2 if i + 2 < n_col else n_col - 1) if i % 2 == 0 else (i - 2 if i > 2 else 0)) for i in range(n_col)]
    def from_turn(value, k):
        return lax.ppermute(value, "row", [(i ^ k if flips else (i + k) % n_row, i) for i in range(n_row)])

    def gather(value, at, forward=None):
        if n_row != 4 or forward is None:
            fields = [value] + [from_turn(value, k) for k in range(1, n_row)]
            return fields, [k * bricks + at for k in range(n_row)]
        one, two = from_turn(value, 1), from_turn(value, 2)
        low, high = one[:forward], two[forward:]
        fields, places = [value, one, two], [at, bricks + at, 2 * bricks + at]
        if low.shape[0]:
            fields, places = fields + [from_turn(low, 2)], places + [3 * bricks + at]
        if high.shape[0]:
            fields, places = fields + [from_turn(high, 1)], places + [3 * bricks + at + forward]
        return fields, places

    own = block if pairs > 1 else 0

    def begin(sums):
        if pairs == 1:
            return [sums, lax.ppermute(sums, "col", swap)]
        lead = lax.ppermute(sums[:block], "col", swap)
        mine = block_of(pairs - 1) * block
        total = small_call(functools.partial(carry_kernel, mine, 0), (block,), "carry", sums, lead)[0]
        later = small_call(tail_kernel, (sums.shape[0] - block,), "tail", sums, after=(total,))[0]
        return [sums, lax.ppermute(later, "col", swap), total]

    def scatter(sums, rest, *total, after=()):
        for distance in range(pairs - 1, 0, -1):
            came = lax.ppermute(total[0], "col", ring)
            if distance == 1:
                kernel = functools.partial(cross_kernel, len(after))
                crossing = small_call(kernel, (half,), "cross", came, after=after)[0]
                return sums, rest, came, lax.ppermute(crossing, "col", swap)
            mine, other = block_of(distance - 1) * block, (block_of(pairs - distance + 1) - 1) * block
            kernel = functools.partial(carry_kernel, mine, other)
            total = small_call(kernel, (block,), "carry", sums, rest, came)
        return sums, rest

    def finish(parts, half_at):
        args = [a for p in parts for a in p]
        kernel = functools.partial(finish_kernel, len(parts), half_at, own)
        return small_call(kernel, (len(parts) * half,), "finish", source, *args)[0]

    plan = make_plan(row_index, col_index, live_count[0], bricks, n_row, n_col, flips)
    matrix = prepare(blocks)
    apply = functools.partial(transfer, plan, matrix)
    senders, out_bricks = n_row * bricks, half * n_col

    fields, at = gather(source, 0)
    sums = apply(fields, at, senders, ((0, 2), (2, 4)), (), out_bricks)
    for _ in range(ITERS - 1):
        chains = [begin(s) for s in sums]
        halves = []
        for h in range(HALVES):
            halves.append(finish([scatter(*chains[h], after=halves)], h))
        near, near_at = gather(halves[0], 0, half)
        far, far_at = gather(halves[1], half, 0)
        sums = apply(near, near_at, senders, ((0, 1), (2, 3)), (), out_bricks)
        sums = apply(far, far_at, senders, ((1, 2), (3, 4)), sums, out_bricks)
    chains = [begin(s) for s in sums]
    return finish([scatter(*chains[h]) for h in range(HALVES)], 0)


def solution(mesh):
    in_specs = (
        P(("row", "col"), None, None),
        P(("row", "col"), None, None),
        P(("row", "col")),
        P(("row", "col")),
        P(("row", "col")),
    )
    out_specs = P(("row", "col"), None, None)
    return jax.shard_map(body, mesh=mesh, in_specs=in_specs, out_specs=out_specs, check_vma=False)
```

```python
import functools

import jax
import jax.numpy as jnp
from jax import lax
from jax.experimental import pallas as pl
from jax.experimental.pallas import tpu as pltpu
from jax.sharding import PartitionSpec as P

ITERS = 2
HALVES = 2
STAGES = 3
GROUP = 32
CHUNK = 16
PLAN_HEAD = 8
MIB = 2**20
SMALL = 2 * MIB
BF16 = jnp.bfloat16
F32 = jnp.float32


def split_parts(value):
    high = value.astype(BF16)
    low = (value - high.astype(F32)).astype(BF16)
    return high, low


def prepare_kernel(b_hbm, o_ref, b_ref, t_ref, sems):
    cells, _, slots = b_hbm.shape
    width = min(128, slots)
    rounds = cells // CHUNK
    copies = [
        pltpu.make_async_copy(b_hbm.at[pl.ds(r * CHUNK, CHUNK)], b_ref.at[pl.ds(r * CHUNK, CHUNK)], sems.at[r])
        for r in range(rounds)
    ]
    for copy in copies:
        copy.start()
    o_ref[slots] = jnp.zeros(o_ref.shape[1:], BF16)
    for r in range(rounds):
        copies[r].wait()

        def turn(i, carry, r=r):
            for c in range(slots // width):
                value = b_ref[r * CHUNK + i, :, pl.ds(c * width, width)]
                high = value.astype(BF16).astype(F32)
                t_ref[i, pl.ds(c * width, width), :] = jnp.concatenate([high, value - high], axis=0).T
            return carry

        lax.fori_loop(0, CHUNK, turn, 0, unroll=4)

        def regroup(g, carry, r=r):
            first = pl.multiple_of(g * 8, 8)
            o_ref[pl.ds(first, 8), pl.ds(r * CHUNK, CHUNK), :] = jnp.swapaxes(t_ref[:, pl.ds(first, 8), :], 0, 1).astype(BF16)
            return carry

        lax.fori_loop(0, slots // 8, regroup, 0, unroll=2)


def prepare(blocks):
    slots, cells, _ = blocks.shape
    return pl.pallas_call(
        prepare_kernel,
        in_specs=[pl.BlockSpec(memory_space=pltpu.HBM)],
        out_specs=pl.BlockSpec(memory_space=pltpu.VMEM),
        out_shape=jax.ShapeDtypeStruct((slots + 1, cells, 2 * cells), BF16),
        scratch_shapes=[
            pltpu.VMEM((cells, cells, slots), F32),
            pltpu.VMEM((CHUNK, slots, 2 * cells), F32),
            pltpu.SemaphoreType.DMA((cells // CHUNK,)),
        ],
        compiler_params=pltpu.CompilerParams(vmem_limit_bytes=14 * MIB),
        cost_estimate=pl.CostEstimate(flops=0, bytes_accessed=24 * MIB, transcendentals=0),
        name="prepare",
    )(pltpu.with_memory_space_constraint(jnp.transpose(blocks, (1, 2, 0)), pltpu.HBM))


def transfer_kernel(fields_at, begin, end, has_before, plan_ref, a_ref, *rest):
    x_refs, (out_ref, w_ref) = rest[: len(fields_at)], rest[-2:]
    zero_slot, cells = a_ref.shape[0] - 1, a_ref.shape[1]
    length = (plan_ref.shape[0] - PLAN_HEAD) // 3
    for x_ref, at in zip(x_refs, fields_at):

        def split_brick(c, carry, x_ref=x_ref, at=at):
            w_ref[at + c] = jnp.concatenate(split_parts(x_ref[c]), axis=0)
            return carry

        lax.fori_loop(0, x_ref.shape[0], split_brick, 0, unroll=True)

    def clear(c, carry):
        out_ref[c] = rest[-3][c] if has_before else jnp.zeros(out_ref.shape[1:], F32)
        return carry

    lax.fori_loop(0, out_ref.shape[0], clear, 0, unroll=4)
    first, last = plan_ref[begin], plan_ref[end]

    def step(g, carry, size, first):
        results, targets = [], []
        for u in range(size):
            s = first + g * size + u
            a = a_ref[jnp.where(s < last, plan_ref[PLAN_HEAD + s], zero_slot)]
            w = w_ref[jnp.where(s < last, plan_ref[PLAN_HEAD + 2 * length + s], fields_at[0])]
            targets.append(plan_ref[PLAN_HEAD + length + s])
            high, low = w[:cells], w[cells:]
            results.append(
                jnp.dot(
                    jnp.concatenate([a, a], axis=1),
                    jnp.concatenate([high, high, low, low], axis=0),
                    preferred_element_type=F32,
                )
            )
        for u in range(size):
            out_ref[targets[u]] += results[u]
        return carry

    large = (last - first + GROUP // 2 - 1) // GROUP
    lax.fori_loop(0, large, functools.partial(step, size=GROUP, first=first), 0)
    rest_first = first + large * GROUP
    small = jnp.where(rest_first < last, 1, 0)
    lax.fori_loop(0, small, functools.partial(step, size=GROUP // 2, first=rest_first), 0)


def transfer(plan, matrix, fields, fields_at, senders, begin, end, before, out_bricks):
    cells, lights = fields[0].shape[1:]
    whole = pl.BlockSpec(memory_space=pltpu.VMEM)
    scratch = senders * 2 * cells * lights * 2
    rows = matrix.shape[0] * cells * (end - begin) // STAGES
    return pl.pallas_call(
        functools.partial(transfer_kernel, fields_at, begin, end, len(before)),
        in_specs=[pl.BlockSpec(memory_space=pltpu.SMEM)] + [whole] * (1 + len(fields) + len(before)),
        out_specs=whole,
        out_shape=jax.ShapeDtypeStruct((out_bricks, cells, lights), F32),
        scratch_shapes=[pltpu.VMEM((senders, 2 * cells, lights), BF16)],
        compiler_params=pltpu.CompilerParams(vmem_limit_bytes=SMALL + scratch),
        cost_estimate=pl.CostEstimate(flops=2 * rows * 4 * cells * lights, bytes_accessed=8 * MIB, transcendentals=0),
        name="transfer",
    )(plan, matrix, *fields, *before)


def first_of_line():
    me, n = lax.axis_index("col"), lax.axis_size("col")
    return jnp.where(me % 2 == 0, me == 0, me == n - 1)


def small_call(kernel, out_bricks, name, *args, after=()):
    whole, anywhere = pl.BlockSpec(memory_space=pltpu.VMEM), pl.BlockSpec(memory_space=pl.ANY)
    shape = args[0].shape[1:]
    return pl.pallas_call(
        kernel,
        in_specs=[whole] * len(args) + [anywhere] * len(after),
        out_specs=[whole] * len(out_bricks),
        out_shape=[jax.ShapeDtypeStruct((n, *shape), F32) for n in out_bricks],
        compiler_params=pltpu.CompilerParams(vmem_limit_bytes=SMALL),
        cost_estimate=pl.CostEstimate(flops=0, bytes_accessed=MIB, transcendentals=0),
        name=name,
    )(*args, *after)


def block_of(distance):
    return {0: 1, 1: 0}.get(distance, distance)


def carry_kernel(mine, other, sums_ref, got_ref, *rest):
    came_refs, out_ref = rest[:-1], rest[-1]
    first = first_of_line()
    for c in range(out_ref.shape[0]):
        total = sums_ref[mine + c] + got_ref[other + c]
        if came_refs:
            total += jnp.where(first, 0.0, came_refs[0][c])
        out_ref[c] = total


def finish_kernel(n_halves, half_at, owns, source_ref, sums_ref, *rest):
    out_ref = rest[-1]
    first = first_of_line()
    per = (len(rest) - 1) // n_halves
    for h in range(n_halves):
        got_ref, *ends = rest[h * per : (h + 1) * per]
        half = out_ref.shape[0] // n_halves
        for c in range(half):
            total = source_ref[(half_at + h) * half + c] + (sums_ref[owns[half_at + h] + c] + got_ref[half + c])
            if ends:
                total += jnp.where(first, 0.0, ends[0][c]) + ends[1][c]
            out_ref[h * half + c] = total


def cross_kernel(came_ref, *rest):
    out_ref = rest[-1]
    half = out_ref.shape[0]
    first = first_of_line()
    for c in range(half):
        out_ref[c] = jnp.where(first, 0.0, came_ref[half + c])


def cut_kernel(at, value_ref, *rest):
    out_ref = rest[-1]
    out_ref[...] = value_ref[at : at + out_ref.shape[0]]


def make_plan(row_index, col_index, live, bricks, n_row, n_col, flips):
    pairs, half = n_col // 2, bricks // HALVES
    my_row, me = lax.axis_index("row"), lax.axis_index("col")
    my_pair, my_side = me // 2, me % 2
    column, brick = row_index // bricks, row_index % bricks
    pair, side = column // 2, column % 2
    ahead = jnp.where(my_side == 0, pair - my_pair, my_pair - pair) % pairs
    ahead = jnp.where(ahead < 2, 1 - ahead, ahead) if pairs > 1 else ahead
    carrier = jnp.where(pair > my_pair, 0, jnp.where(pair < my_pair, 1, my_side))
    place = ((brick // half * pairs + ahead) * 2 + (side ^ carrier)) * half + brick % half

    from_row, from_brick = col_index // bricks, col_index % bricks
    turn = from_row ^ my_row if flips else (from_row - my_row) % n_row
    sender = turn * bricks + from_brick

    n = row_index.shape[0]
    slots = jnp.arange(n, dtype=jnp.int32)
    part = jnp.where(turn == 0, 0, jnp.where(turn < n_row - 1, 1, 2))
    part = jnp.where(slots < live, part, STAGES)
    key = part * n + slots
    rank = jnp.sum(key[None, :] < key[:, None], axis=1, dtype=jnp.int32)
    chosen = rank[None, :] == jnp.arange(n + GROUP, dtype=jnp.int32)[:, None]

    def in_order(value):
        return jnp.sum(jnp.where(chosen, value[None, :], 0), axis=1, dtype=jnp.int32)

    bounds = jnp.arange(PLAN_HEAD, dtype=jnp.int32)
    starts = jnp.sum(part[None, :] < bounds[:, None], axis=1, dtype=jnp.int32)
    return jnp.concatenate([starts, in_order(slots), in_order(place), in_order(sender)])


def body(source, blocks, row_index, col_index, live_count):
    bricks = source.shape[0]
    n_row, n_col = lax.axis_size("row"), lax.axis_size("col")
    pairs, half = n_col // 2, bricks // HALVES
    block = 2 * half
    flips = n_row & (n_row - 1) == 0

    swap = [(i, i ^ 1) for i in range(n_col)]
    ring = [(i, (i + 2 if i + 2 < n_col else n_col - 1) if i % 2 == 0 else (i - 2 if i > 2 else 0)) for i in range(n_col)]
    def from_turn(value, k):
        return lax.ppermute(value, "row", [(i ^ k if flips else (i + k) % n_row, i) for i in range(n_row)])

    def gather(values, direct):
        return [[from_turn(v, k) for v in values] for k in range(1, n_row if direct else n_row - 1)]

    def cut(value, at, size, after):
        return small_call(functools.partial(cut_kernel, at), (size,), "cut", value, after=after)[0]

    def forward(value, k, *after):
        return from_turn(cut(value, 0, value.shape[0], after), k)

    def apply(turns, first, end, *before):
        fields = [f for pieces in turns.values() for f in pieces]
        at = [k * bricks + i * (bricks // len(pieces)) for k, pieces in turns.items() for i in range(len(pieces))]
        return transfer(plan, matrix, fields, at, n_row * bricks, first, end, before, bricks * n_col)

    in_half = half * n_col
    owns = [h * in_half + (block if pairs > 1 else 0) for h in range(HALVES)]

    def begin(sums, h):
        base = h * in_half
        if pairs == 1:
            return [base, lax.ppermute(sums[base : base + in_half], "col", swap)]
        lead = lax.ppermute(sums[base : base + block], "col", swap)
        mine = base + block_of(pairs - 1) * block
        total = small_call(functools.partial(carry_kernel, mine, 0), (block,), "carry", sums, lead)[0]
        later = cut(sums, base + block, in_half - block, (total,))
        return [base, lax.ppermute(later, "col", swap), total]

    def scatter(sums, base, rest, *total, after=()):
        for distance in range(pairs - 1, 0, -1):
            came = lax.ppermute(total[0], "col", ring)
            if distance == 1:
                crossing = small_call(cross_kernel, (half,), "cross", came, after=after)[0]
                return rest, came, lax.ppermute(crossing, "col", swap)
            mine, other = base + block_of(distance - 1) * block, (block_of(pairs - distance + 1) - 1) * block
            kernel = functools.partial(carry_kernel, mine, other)
            total = small_call(kernel, (block,), "carry", sums, rest, came)
        return (rest,)

    def finish(sums, parts, half_at):
        args = [a for p in parts for a in p]
        kernel = functools.partial(finish_kernel, len(parts), half_at, owns)
        return small_call(kernel, (len(parts) * half,), "finish", source, sums, *args)[0]

    plan = make_plan(row_index, col_index, live_count[0], bricks, n_row, n_col, flips)
    matrix = prepare(blocks)

    others = gather([source], True)
    sums = apply({0: [source]}, 0, 1)
    sums = apply(dict(enumerate(others, 1)), 1, STAGES, sums)
    for _ in range(ITERS - 1):
        chains = [begin(sums, h) for h in range(HALVES)]
        field = []
        for h in range(HALVES):
            field.append(finish(sums, [scatter(sums, *chains[h], after=field)], h))
        sums = apply({0: field}, 0, 1)
        if n_row == 4:
            one, two = gather(field, False)
            last = [forward(one[0], 2, two[0], sums), forward(two[1], 1, one[1])]
            sums = apply({1: one, 2: two}, 1, 2, sums)
            sums = apply({3: last}, 2, STAGES, sums)
        else:
            sums = apply(dict(enumerate(gather(field, True), 1)), 1, STAGES, sums)
    chains = [begin(sums, h) for h in range(HALVES)]
    return finish(sums, [scatter(sums, *c) for c in chains], 0)


def solution(mesh):
    in_specs = (
        P(("row", "col"), None, None),
        P(("row", "col"), None, None),
        P(("row", "col")),
        P(("row", "col")),
        P(("row", "col")),
    )
    out_specs = P(("row", "col"), None, None)
    return jax.shard_map(body, mesh=mesh, in_specs=in_specs, out_specs=out_specs, check_vma=False)
```

```python
import functools

import jax
import jax.numpy as jnp
from jax import lax
from jax.experimental import pallas as pl
from jax.experimental.pallas import tpu as pltpu
from jax.sharding import PartitionSpec as P

ITERS = 2
HALVES = 2
STAGES = 3
GROUP = 32
CHUNK = 16
PLAN_HEAD = 8
MIB = 2**20
SMALL = 2 * MIB
BF16 = jnp.bfloat16
F32 = jnp.float32


def split_parts(value):
    high = value.astype(BF16)
    low = (value - high.astype(F32)).astype(BF16)
    return high, low


def prepare_kernel(b_hbm, o_ref, b_ref, t_ref, sems):
    cells, _, slots = b_hbm.shape
    middle, width = cells // 2, min(128, slots)
    copies = []
    for r in range(middle // CHUNK):
        for side in range(2):
            rows = pl.ds(side * middle + r * CHUNK, CHUNK)
            copies.append(pltpu.make_async_copy(b_hbm.at[rows], b_ref.at[rows], sems.at[2 * r + side]))
    for copy in copies:
        copy.start()
    o_ref[slots] = jnp.zeros(o_ref.shape[1:], BF16)
    for r in range(middle // CHUNK):
        copies[2 * r].wait()
        copies[2 * r + 1].wait()

        def turn(i, carry, r=r):
            for c in range(slots // width):
                first, second = [b_ref[side * middle + r * CHUNK + i, :, pl.ds(c * width, width)] for side in range(2)]
                t_ref[i, pl.ds(c * width, width), :] = jnp.concatenate([first, second], axis=0).T
            return carry

        lax.fori_loop(0, CHUNK, turn, 0, unroll=True)

        def regroup(g, carry, r=r):
            first = pl.multiple_of(g * 8, 8)
            value = jnp.swapaxes(t_ref[:, pl.ds(first, 8), :], 0, 1)
            other = pltpu.roll(value, cells, 2)
            left = lax.broadcasted_iota(jnp.int32, value.shape, 2) < cells
            value_high, other_high = value.astype(BF16).astype(F32), other.astype(BF16).astype(F32)
            upper = jnp.where(left, value_high, other - other_high)
            lower = jnp.where(left, other_high, value - value_high)
            o_ref[pl.ds(first, 8), pl.ds(r * CHUNK, CHUNK), :] = upper.astype(BF16)
            o_ref[pl.ds(first, 8), pl.ds(middle + r * CHUNK, CHUNK), :] = lower.astype(BF16)
            return carry

        lax.fori_loop(0, slots // 8, regroup, 0, unroll=True)


def prepare(blocks):
    slots, cells, _ = blocks.shape
    return pl.pallas_call(
        prepare_kernel,
        in_specs=[pl.BlockSpec(memory_space=pltpu.HBM)],
        out_specs=pl.BlockSpec(memory_space=pltpu.VMEM),
        out_shape=jax.ShapeDtypeStruct((slots + 1, cells, 2 * cells), BF16),
        scratch_shapes=[
            pltpu.VMEM((cells, cells, slots), F32),
            pltpu.VMEM((CHUNK, slots, 2 * cells), F32),
            pltpu.SemaphoreType.DMA((cells // CHUNK,)),
        ],
        compiler_params=pltpu.CompilerParams(vmem_limit_bytes=14 * MIB),
        cost_estimate=pl.CostEstimate(flops=0, bytes_accessed=24 * MIB, transcendentals=0),
        name="prepare",
    )(pltpu.with_memory_space_constraint(jnp.transpose(blocks, (1, 2, 0)), pltpu.HBM))


def transfer_kernel(fields_at, begin, end, has_before, plan_ref, a_ref, *rest):
    x_refs, (out_ref, w_ref) = rest[: len(fields_at)], rest[-2:]
    zero_slot, cells = a_ref.shape[0] - 1, a_ref.shape[1]
    length = (plan_ref.shape[0] - PLAN_HEAD) // 3
    for x_ref, at in zip(x_refs, fields_at):

        def split_brick(c, carry, x_ref=x_ref, at=at):
            w_ref[at + c] = jnp.concatenate(split_parts(x_ref[c]), axis=0)
            return carry

        lax.fori_loop(0, x_ref.shape[0], split_brick, 0, unroll=True)

    def clear(c, carry):
        out_ref[c] = rest[-3][c] if has_before else jnp.zeros(out_ref.shape[1:], F32)
        return carry

    lax.fori_loop(0, out_ref.shape[0], clear, 0, unroll=4)
    first, last = plan_ref[begin], plan_ref[end]

    def step(g, carry, size, first):
        results, targets = [], []
        for u in range(size):
            s = first + g * size + u
            a = a_ref[jnp.where(s < last, plan_ref[PLAN_HEAD + s], zero_slot)]
            w = w_ref[jnp.where(s < last, plan_ref[PLAN_HEAD + 2 * length + s], fields_at[0])]
            targets.append(plan_ref[PLAN_HEAD + length + s])
            high, low = w[:cells], w[cells:]
            results.append(
                jnp.dot(
                    jnp.concatenate([a, a], axis=1),
                    jnp.concatenate([high, high, low, low], axis=0),
                    preferred_element_type=F32,
                )
            )
        for u in range(size):
            out_ref[targets[u]] += results[u]
        return carry

    large = (last - first + GROUP // 2 - 1) // GROUP
    lax.fori_loop(0, large, functools.partial(step, size=GROUP, first=first), 0)
    rest_first = first + large * GROUP
    small = jnp.where(rest_first < last, 1, 0)
    lax.fori_loop(0, small, functools.partial(step, size=GROUP // 2, first=rest_first), 0)


def transfer(plan, matrix, fields, fields_at, senders, begin, end, before, out_bricks):
    cells, lights = fields[0].shape[1:]
    whole = pl.BlockSpec(memory_space=pltpu.VMEM)
    scratch = senders * 2 * cells * lights * 2
    rows = matrix.shape[0] * cells * (end - begin) // STAGES
    return pl.pallas_call(
        functools.partial(transfer_kernel, fields_at, begin, end, len(before)),
        in_specs=[pl.BlockSpec(memory_space=pltpu.SMEM)] + [whole] * (1 + len(fields) + len(before)),
        out_specs=whole,
        out_shape=jax.ShapeDtypeStruct((out_bricks, cells, lights), F32),
        scratch_shapes=[pltpu.VMEM((senders, 2 * cells, lights), BF16)],
        compiler_params=pltpu.CompilerParams(vmem_limit_bytes=SMALL + scratch),
        cost_estimate=pl.CostEstimate(flops=0, bytes_accessed=0, transcendentals=0),
        name="transfer",
    )(pltpu.with_memory_space_constraint(plan, pltpu.SMEM), matrix, *fields, *before)


def keep_kernel(value_ref, out_ref, sem):
    copy = pltpu.make_async_copy(value_ref, out_ref, sem)
    copy.start()
    copy.wait()


def in_scalar_memory(value):
    return pl.pallas_call(
        keep_kernel,
        in_specs=[pl.BlockSpec(memory_space=pltpu.VMEM)],
        out_specs=pl.BlockSpec(memory_space=pltpu.SMEM),
        out_shape=pltpu.SMEM(value.shape, value.dtype),
        scratch_shapes=[pltpu.SemaphoreType.DMA],
        compiler_params=pltpu.CompilerParams(vmem_limit_bytes=SMALL),
        name="keep",
    )(value)


def first_of_line():
    me, n = lax.axis_index("col"), lax.axis_size("col")
    return jnp.where(me % 2 == 0, me == 0, me == n - 1)


def small_call(kernel, out_bricks, name, *args, after=()):
    whole, anywhere = pl.BlockSpec(memory_space=pltpu.VMEM), pl.BlockSpec(memory_space=pl.ANY)
    shape = args[0].shape[1:]
    return pl.pallas_call(
        kernel,
        in_specs=[whole] * len(args) + [anywhere] * len(after),
        out_specs=[whole] * len(out_bricks),
        out_shape=[jax.ShapeDtypeStruct((n, *shape), F32) for n in out_bricks],
        compiler_params=pltpu.CompilerParams(vmem_limit_bytes=SMALL),
        cost_estimate=pl.CostEstimate(flops=0, bytes_accessed=0, transcendentals=0),
        name=name,
    )(*args, *after)


def block_of(distance):
    return {0: 1, 1: 0}.get(distance, distance)


def carry_kernel(mine, other, sums_ref, got_ref, *rest):
    came_refs, out_ref = rest[:-1], rest[-1]
    first = first_of_line()
    for c in range(out_ref.shape[0]):
        total = sums_ref[mine + c] + got_ref[other + c]
        if came_refs:
            total += jnp.where(first, 0.0, came_refs[0][c])
        out_ref[c] = total


def finish_kernel(n_halves, half_at, owns, source_ref, sums_ref, *rest):
    out_ref = rest[-1]
    first = first_of_line()
    per = (len(rest) - 1) // n_halves
    for h in range(n_halves):
        got_ref, *ends = rest[h * per : (h + 1) * per]
        half = out_ref.shape[0] // n_halves
        for c in range(half):
            total = source_ref[(half_at + h) * half + c] + (sums_ref[owns[half_at + h] + c] + got_ref[half + c])
            if ends:
                total += jnp.where(first, 0.0, ends[0][c]) + ends[1][c]
            out_ref[h * half + c] = total


def cross_kernel(came_ref, *rest):
    out_ref = rest[-1]
    half, first = out_ref.shape[0], first_of_line()
    for c in range(half):
        out_ref[c] = jnp.where(first, 0.0, came_ref[half + c])


def cut_kernel(at, value_ref, *rest):
    out_ref = rest[-1]
    out_ref[...] = value_ref[at : at + out_ref.shape[0]]


def make_plan(row_index, col_index, live, bricks, n_row, n_col, flips):
    pairs, half = n_col // 2, bricks // HALVES
    my_row, me = lax.axis_index("row"), lax.axis_index("col")
    my_pair, my_side = me // 2, me % 2
    column, brick = row_index // bricks, row_index % bricks
    pair, side = column // 2, column % 2
    ahead = jnp.where(my_side == 0, pair - my_pair, my_pair - pair) % pairs
    ahead = jnp.where(ahead < 2, 1 - ahead, ahead) if pairs > 1 else ahead
    carrier = jnp.where(pair > my_pair, 0, jnp.where(pair < my_pair, 1, my_side))
    place = ((brick // half * pairs + ahead) * 2 + (side ^ carrier)) * half + brick % half

    from_row, from_brick = col_index // bricks, col_index % bricks
    turn = from_row ^ my_row if flips else (from_row - my_row) % n_row
    sender = turn * bricks + from_brick

    n = row_index.shape[0]
    slots = jnp.arange(n, dtype=jnp.int32)
    part = jnp.where(turn == 0, 0, jnp.where(turn < n_row - 1, 1, 2))
    part = jnp.where(slots < live, part, STAGES)
    key = part * n + slots
    rank = jnp.sum(key[None, :] < key[:, None], axis=1, dtype=jnp.int32)
    chosen = rank[None, :] == jnp.arange(n + GROUP, dtype=jnp.int32)[:, None]

    def in_order(value):
        return jnp.sum(jnp.where(chosen, value[None, :], 0), axis=1, dtype=jnp.int32)

    bounds = jnp.arange(PLAN_HEAD, dtype=jnp.int32)
    starts = jnp.sum(part[None, :] < bounds[:, None], axis=1, dtype=jnp.int32)
    return jnp.concatenate([starts, in_order(slots), in_order(place), in_order(sender)])


def body(source, blocks, row_index, col_index, live_count):
    bricks = source.shape[0]
    n_row, n_col = lax.axis_size("row"), lax.axis_size("col")
    pairs, half = n_col // 2, bricks // HALVES
    block = 2 * half
    flips = n_row & (n_row - 1) == 0

    swap = [(i, i ^ 1) for i in range(n_col)]
    ring = [(i, (i + 2 if i + 2 < n_col else n_col - 1) if i % 2 == 0 else (i - 2 if i > 2 else 0)) for i in range(n_col)]

    def from_turn(value, k):
        return lax.ppermute(value, "row", [(i ^ k if flips else (i + k) % n_row, i) for i in range(n_row)])

    def gather(values, direct):
        return [[from_turn(v, k) for v in values] for k in range(1, n_row if direct else n_row - 1)]

    def cut(value, at, size, after):
        return small_call(functools.partial(cut_kernel, at), (size,), "cut", value, after=after)[0]

    def forward(value, k, *after):
        return from_turn(cut(value, 0, value.shape[0], after), k)

    def apply(turns, first, end, *before):
        fields = [f for pieces in turns.values() for f in pieces]
        at = [k * bricks + i * (bricks // len(pieces)) for k, pieces in turns.items() for i in range(len(pieces))]
        return transfer(plan, matrix, fields, at, n_row * bricks, first, end, before, bricks * n_col)

    in_half = half * n_col
    owns = [h * in_half + (block if pairs > 1 else 0) for h in range(HALVES)]

    def begin(sums, h):
        base = h * in_half
        if pairs == 1:
            return base, None, lax.ppermute(sums[base : base + in_half], "col", swap)
        lead = lax.ppermute(sums[base : base + block], "col", swap)
        mine = base + block_of(pairs - 1) * block
        total = small_call(functools.partial(carry_kernel, mine, 0), (block,), "carry", sums, lead)[0]
        later = cut(sums, base + block, in_half - block, (total,))
        return base, total, lax.ppermute(later, "col", swap)

    def total_for(sums, base, rest, distance, came):
        mine, other = base + block_of(distance) * block, (block_of(pairs - distance) - 1) * block
        return small_call(functools.partial(carry_kernel, mine, other), (block,), "carry", sums, rest, came)[0]

    def scatter(sums):
        parts = []
        for base, total, rest in [begin(sums, h) for h in range(HALVES)]:
            parts.append([rest])
            if pairs > 1:
                came = lax.ppermute(total, "col", ring)
                for distance in range(pairs - 2, 0, -1):
                    came = lax.ppermute(total_for(sums, base, rest, distance, came), "col", ring)
                parts[-1].append(came)
        return parts

    def finish(sums, parts, half_at, after=()):
        args = []
        for rest, *came in parts:
            args += [rest, *came]
            if came:
                crossing = small_call(cross_kernel, (half,), "cross", *came, after=after)[0]
                args.append(lax.ppermute(crossing, "col", swap))
        kernel = functools.partial(finish_kernel, len(parts), half_at, owns)
        return small_call(kernel, (len(parts) * half,), "finish", source, sums, *args)[0]

    plan = in_scalar_memory(make_plan(row_index, col_index, live_count[0], bricks, n_row, n_col, flips))
    matrix = prepare(blocks)

    if n_row == 4:
        one, two = gather([source], False)
        last = [forward(one[0][:half], 2, two[0], matrix), forward(two[0][half:], 1, one[0], matrix)]
        sums = apply({0: [source], 1: one, 2: two}, 0, 2)
        sums = apply({3: last}, 2, STAGES, sums)
    else:
        sums = apply(dict(enumerate([[source], *gather([source], True)])), 0, STAGES)
    for _ in range(ITERS - 1):
        field = []
        for h, part in enumerate(scatter(sums)):
            field.append(finish(sums, [part], h, field))
        sums = apply({0: field}, 0, 1)
        if n_row == 4:
            one, two = gather(field, False)
            last = [forward(one[0], 2, two[0], sums), forward(two[1], 1, one[1])]
            sums = apply({1: one, 2: two}, 1, 2, sums)
            sums = apply({3: last}, 2, STAGES, sums)
        else:
            sums = apply(dict(enumerate(gather(field, True), 1)), 1, STAGES, sums)
    return finish(sums, scatter(sums), 0)


def solution(mesh):
    in_specs = (
        P(("row", "col"), None, None),
        P(("row", "col"), None, None),
        P(("row", "col")),
        P(("row", "col")),
        P(("row", "col")),
    )
    out_specs = P(("row", "col"), None, None)
    return jax.shard_map(body, mesh=mesh, in_specs=in_specs, out_specs=out_specs, check_vma=False)
```

```python
import functools

import jax
import jax.numpy as jnp
from jax import lax
from jax.experimental import pallas as pl
from jax.experimental.pallas import tpu as pltpu
from jax.sharding import PartitionSpec as P

ITERS = 2
HALVES = 2
STAGES = 4
GROUP = 32
CHUNK = 16
PLAN_HEAD = 8
MIB = 2**20
SMALL = 2 * MIB
BF16 = jnp.bfloat16
F32 = jnp.float32


def split_parts(value):
    high = value.astype(BF16)
    low = (value - high.astype(F32)).astype(BF16)
    return high, low


def prepare_kernel(b_hbm, o_ref, b_ref, t_ref, sems):
    cells, _, slots = b_hbm.shape
    middle, width = cells // 2, min(128, slots)
    copies = []
    for r in range(middle // CHUNK):
        for side in range(2):
            rows = pl.ds(side * middle + r * CHUNK, CHUNK)
            copies.append(pltpu.make_async_copy(b_hbm.at[rows], b_ref.at[rows], sems.at[2 * r + side]))
    for copy in copies:
        copy.start()
    o_ref[slots] = jnp.zeros(o_ref.shape[1:], BF16)
    for r in range(middle // CHUNK):
        copies[2 * r].wait()
        copies[2 * r + 1].wait()

        def turn(i, carry, r=r):
            for c in range(slots // width):
                first, second = [b_ref[side * middle + r * CHUNK + i, :, pl.ds(c * width, width)] for side in range(2)]
                t_ref[i, pl.ds(c * width, width), :] = jnp.concatenate([first, second], axis=0).T
            return carry

        lax.fori_loop(0, CHUNK, turn, 0, unroll=True)

        def regroup(g, carry, r=r):
            first = pl.multiple_of(g * 8, 8)
            value = jnp.swapaxes(t_ref[:, pl.ds(first, 8), :], 0, 1)
            other = pltpu.roll(value, cells, 2)
            left = lax.broadcasted_iota(jnp.int32, value.shape, 2) < cells
            value_high, other_high = value.astype(BF16).astype(F32), other.astype(BF16).astype(F32)
            upper = jnp.where(left, value_high, other - other_high)
            lower = jnp.where(left, other_high, value - value_high)
            o_ref[pl.ds(first, 8), pl.ds(r * CHUNK, CHUNK), :] = upper.astype(BF16)
            o_ref[pl.ds(first, 8), pl.ds(middle + r * CHUNK, CHUNK), :] = lower.astype(BF16)
            return carry

        lax.fori_loop(0, slots // 8, regroup, 0, unroll=True)


def prepare(blocks):
    slots, cells, _ = blocks.shape
    return pl.pallas_call(
        prepare_kernel,
        in_specs=[pl.BlockSpec(memory_space=pltpu.HBM)],
        out_specs=pl.BlockSpec(memory_space=pltpu.VMEM),
        out_shape=jax.ShapeDtypeStruct((slots + 1, cells, 2 * cells), BF16),
        scratch_shapes=[
            pltpu.VMEM((cells, cells, slots), F32),
            pltpu.VMEM((CHUNK, slots, 2 * cells), F32),
            pltpu.SemaphoreType.DMA((cells // CHUNK,)),
        ],
        compiler_params=pltpu.CompilerParams(vmem_limit_bytes=14 * MIB),
        cost_estimate=pl.CostEstimate(flops=0, bytes_accessed=24 * MIB, transcendentals=0),
        name="prepare",
    )(pltpu.with_memory_space_constraint(jnp.transpose(blocks, (1, 2, 0)), pltpu.HBM))


def transfer_kernel(fields_at, begin, end, has_before, plan_ref, a_ref, *rest):
    x_refs, (out_ref, w_ref) = rest[: len(fields_at)], rest[-2:]
    zero_slot, cells = a_ref.shape[0] - 1, a_ref.shape[1]
    length = (plan_ref.shape[0] - PLAN_HEAD) // 3
    for x_ref, at in zip(x_refs, fields_at):

        def split_brick(c, carry, x_ref=x_ref, at=at):
            w_ref[at + c] = jnp.concatenate(split_parts(x_ref[c]), axis=0)
            return carry

        lax.fori_loop(0, x_ref.shape[0], split_brick, 0, unroll=True)

    def clear(c, carry):
        out_ref[c] = rest[-3][c] if has_before else jnp.zeros(out_ref.shape[1:], F32)
        return carry

    lax.fori_loop(0, out_ref.shape[0], clear, 0, unroll=4)
    first, last = plan_ref[begin], plan_ref[end]

    def step(g, carry, size, first):
        results, targets = [], []
        for u in range(size):
            s = first + g * size + u
            a = a_ref[jnp.where(s < last, plan_ref[PLAN_HEAD + s], zero_slot)]
            w = w_ref[jnp.where(s < last, plan_ref[PLAN_HEAD + 2 * length + s], fields_at[0])]
            targets.append(plan_ref[PLAN_HEAD + length + s])
            high, low = w[:cells], w[cells:]
            results.append(
                jnp.dot(
                    jnp.concatenate([a, a], axis=1),
                    jnp.concatenate([high, high, low, low], axis=0),
                    preferred_element_type=F32,
                )
            )
        for u in range(size):
            out_ref[targets[u]] += results[u]
        return carry

    large = (last - first + GROUP // 2 - 1) // GROUP
    lax.fori_loop(0, large, functools.partial(step, size=GROUP, first=first), 0)
    rest_first = first + large * GROUP
    small = jnp.where(rest_first < last, 1, 0)
    lax.fori_loop(0, small, functools.partial(step, size=GROUP // 2, first=rest_first), 0)


def transfer(plan, matrix, fields, fields_at, senders, begin, end, before, out_bricks):
    cells, lights = fields[0].shape[1:]
    whole = pl.BlockSpec(memory_space=pltpu.VMEM)
    scratch = senders * 2 * cells * lights * 2
    rows = matrix.shape[0] * cells * (end - begin) // STAGES
    return pl.pallas_call(
        functools.partial(transfer_kernel, fields_at, begin, end, len(before)),
        in_specs=[pl.BlockSpec(memory_space=pltpu.SMEM)] + [whole] * (1 + len(fields) + len(before)),
        out_specs=whole,
        out_shape=jax.ShapeDtypeStruct((out_bricks, cells, lights), F32),
        scratch_shapes=[pltpu.VMEM((senders, 2 * cells, lights), BF16)],
        compiler_params=pltpu.CompilerParams(vmem_limit_bytes=SMALL + scratch),
        cost_estimate=pl.CostEstimate(flops=0, bytes_accessed=0, transcendentals=0),
        name="transfer",
    )(pltpu.with_memory_space_constraint(plan, pltpu.SMEM), matrix, *fields, *before)


def keep_kernel(value_ref, out_ref, sem):
    copy = pltpu.make_async_copy(value_ref, out_ref, sem)
    copy.start()
    copy.wait()


def in_scalar_memory(value):
    return pl.pallas_call(
        keep_kernel,
        in_specs=[pl.BlockSpec(memory_space=pltpu.VMEM)],
        out_specs=pl.BlockSpec(memory_space=pltpu.SMEM),
        out_shape=pltpu.SMEM(value.shape, value.dtype),
        scratch_shapes=[pltpu.SemaphoreType.DMA],
        compiler_params=pltpu.CompilerParams(vmem_limit_bytes=SMALL),
        name="keep",
    )(value)


def first_of_line():
    me, n = lax.axis_index("col"), lax.axis_size("col")
    return jnp.where(me % 2 == 0, me == 0, me == n - 1)


def small_call(kernel, out_bricks, name, *args, after=()):
    whole, anywhere = pl.BlockSpec(memory_space=pltpu.VMEM), pl.BlockSpec(memory_space=pl.ANY)
    shape = args[0].shape[1:]
    return pl.pallas_call(
        kernel,
        in_specs=[whole] * len(args) + [anywhere] * len(after),
        out_specs=[whole] * len(out_bricks),
        out_shape=[jax.ShapeDtypeStruct((n, *shape), F32) for n in out_bricks],
        compiler_params=pltpu.CompilerParams(vmem_limit_bytes=SMALL),
        cost_estimate=pl.CostEstimate(flops=0, bytes_accessed=0, transcendentals=0),
        name=name,
    )(*args, *after)


def carry_kernel(mine, other, sums_ref, got_ref, *rest):
    came_refs, out_ref = rest[:-1], rest[-1]
    first = first_of_line()
    for c in range(out_ref.shape[0]):
        total = sums_ref[mine + c] + got_ref[other + c]
        if came_refs:
            total += jnp.where(first, 0.0, came_refs[0][c])
        out_ref[c] = total


def finish_kernel(half_at, owns, skipped, source_ref, sums_ref, *rest):
    out_ref = rest[-1]
    first = first_of_line()
    per = (len(rest) - 1) // len(owns)
    for h, own in enumerate(owns):
        got_ref, *ends = rest[h * per : (h + 1) * per]
        half = out_ref.shape[0] // len(owns)
        for c in range(half):
            total = source_ref[(half_at + h) * half + c] + (sums_ref[own + c] + got_ref[own - skipped + half + c])
            if ends:
                total += jnp.where(first, 0.0, ends[0][c]) + ends[1][c]
            out_ref[h * half + c] = total


def cross_kernel(came_ref, *rest):
    out_ref = rest[-1]
    half, first = out_ref.shape[0], first_of_line()
    for c in range(half):
        out_ref[c] = jnp.where(first, 0.0, came_ref[half + c])


def cut_kernel(at, value_ref, *rest):
    out_ref = rest[-1]
    out_ref[...] = value_ref[at : at + out_ref.shape[0]]


def sums_at(h, distance, pairs, half):
    order = (distance + pairs - 1) % pairs if pairs > 1 else distance
    size = 2 * half
    return jnp.where(order == 0, h * size, (HALVES + h * (pairs - 1) + order - 1) * size)


def make_plan(row_index, col_index, live, bricks, n_row, n_col, flips):
    pairs, half = n_col // 2, bricks // HALVES
    my_row, me = lax.axis_index("row"), lax.axis_index("col")
    my_pair, my_side = me // 2, me % 2
    column, brick = row_index // bricks, row_index % bricks
    pair, side = column // 2, column % 2
    ahead = jnp.where(my_side == 0, pair - my_pair, my_pair - pair) % pairs
    carrier = jnp.where(pair > my_pair, 0, jnp.where(pair < my_pair, 1, my_side))
    place = sums_at(brick // half, ahead, pairs, half) + (side ^ carrier) * half + brick % half

    from_row, from_brick = col_index // bricks, col_index % bricks
    turn = from_row ^ my_row if flips else (from_row - my_row) % n_row
    sender = turn * bricks + from_brick

    n = row_index.shape[0]
    slots = jnp.arange(n, dtype=jnp.int32)
    part = jnp.where(turn == 0, 0, jnp.where(turn < n_row - 1, 1, jnp.where(place < HALVES * 2 * half, 2, 3)))
    part = jnp.where(slots < live, part, STAGES)
    key = part * n + slots
    rank = jnp.sum(key[None, :] < key[:, None], axis=1, dtype=jnp.int32)
    chosen = rank[None, :] == jnp.arange(n + GROUP, dtype=jnp.int32)[:, None]

    def in_order(value):
        return jnp.sum(jnp.where(chosen, value[None, :], 0), axis=1, dtype=jnp.int32)

    bounds = jnp.arange(PLAN_HEAD, dtype=jnp.int32)
    starts = jnp.sum(part[None, :] < bounds[:, None], axis=1, dtype=jnp.int32)
    return jnp.concatenate([starts, in_order(slots), in_order(place), in_order(sender)])


def body(source, blocks, row_index, col_index, live_count):
    bricks = source.shape[0]
    n_row, n_col = lax.axis_size("row"), lax.axis_size("col")
    pairs, half = n_col // 2, bricks // HALVES
    block = 2 * half
    flips = n_row & (n_row - 1) == 0

    swap = [(i, i ^ 1) for i in range(n_col)]
    ring = [(i, (i + 2 if i + 2 < n_col else n_col - 1) if i % 2 == 0 else (i - 2 if i > 2 else 0)) for i in range(n_col)]

    def from_turn(value, k):
        return lax.ppermute(value, "row", [(i ^ k if flips else (i + k) % n_row, i) for i in range(n_row)])

    def gather(values, direct):
        return [[from_turn(v, k) for v in values] for k in range(1, n_row if direct else n_row - 1)]

    def cut(value, at, size, after):
        return small_call(functools.partial(cut_kernel, at), (size,), "cut", value, after=after)[0]

    def forward(value, k, *after):
        return from_turn(cut(value, 0, value.shape[0], after), k)

    def apply(turns, first, end, *before):
        fields = [f for pieces in turns.values() for f in pieces]
        at = [k * bricks + i * (bricks // len(pieces)) for k, pieces in turns.items() for i in range(len(pieces))]
        return transfer(plan, matrix, fields, at, n_row * bricks, first, end, before, bricks * n_col)

    leading = HALVES * block

    def at(h, distance):
        order = (distance + pairs - 1) % pairs
        return h * block if order == 0 else leading + (h * (pairs - 1) + order - 1) * block

    def scatter(lead, sums):
        first = lax.ppermute(lead[:leading], "col", swap)
        if pairs == 1:
            return [[first]] * HALVES
        far = pairs - 1
        totals = []
        for h in range(HALVES):
            kernel = functools.partial(carry_kernel, at(h, far), h * block)
            totals += small_call(kernel, (block,), "carry", sums, first)
        rest = lax.ppermute(cut(sums, leading, sums.shape[0] - leading, totals), "col", swap)
        parts = []
        for h in range(HALVES):
            came = lax.ppermute(totals[h], "col", ring)
            for distance in range(far - 1, 0, -1):
                kernel = functools.partial(carry_kernel, at(h, distance), at(h, pairs - distance) - leading)
                total = small_call(kernel, (block,), "carry", sums, rest, came)[0]
                came = lax.ppermute(total, "col", ring)
            parts.append([rest, came])
        return parts

    def finish(sums, parts, half_at, after=()):
        args = []
        for rest, *came in parts:
            args += [rest, *came]
            if came:
                crossing = small_call(cross_kernel, (half,), "cross", *came, after=after)[0]
                args.append(lax.ppermute(crossing, "col", swap))
        owns = [at(half_at + h, 0) for h in range(len(parts))]
        kernel = functools.partial(finish_kernel, half_at, owns, leading if pairs > 1 else 0)
        return small_call(kernel, (len(parts) * half,), "finish", source, sums, *args)[0]

    plan = in_scalar_memory(make_plan(row_index, col_index, live_count[0], bricks, n_row, n_col, flips))
    matrix = prepare(blocks)

    def by_row(field):
        return dict(enumerate([field, *gather(field, True)]))

    def last_row(last, sums):
        lead = apply({3: last}, 2, 3, sums)
        return lead, apply({3: last}, 3, STAGES, lead)

    if n_row == 4:
        one, two = gather([source], False)
        last = [forward(one[0][:half], 2, matrix), forward(two[0][half:], 1, matrix)]
        lead, sums = last_row(last, apply({0: [source], 1: one, 2: two}, 0, 2))
    else:
        lead = sums = apply(by_row([source]), 0, STAGES)
    for _ in range(ITERS - 1):
        field = []
        for h, part in enumerate(scatter(lead, sums)):
            field.append(finish(sums, [part], h, field))
        if n_row == 4:
            one, two = gather(field, False)
            sums = apply({0: field}, 0, 1)
            last = [forward(one[0], 2), forward(two[1], 1, sums)]
            lead, sums = last_row(last, apply({1: one, 2: two}, 1, 2, sums))
        else:
            lead = sums = apply(by_row(field), 0, STAGES)
    return finish(sums, scatter(lead, sums), 0)


def solution(mesh):
    in_specs = (
        P(("row", "col"), None, None),
        P(("row", "col"), None, None),
        P(("row", "col")),
        P(("row", "col")),
        P(("row", "col")),
    )
    out_specs = P(("row", "col"), None, None)
    return jax.shard_map(body, mesh=mesh, in_specs=in_specs, out_specs=out_specs, check_vma=False)
```

```python
import functools

import jax
import jax.numpy as jnp
from jax import lax
from jax.experimental import pallas as pl
from jax.experimental.pallas import tpu as pltpu
from jax.sharding import PartitionSpec as P

ITERS = 2
PARTS = 4
GROUPS = (0, 2), (2, 4)
STAGES = 4
GROUP = 32
CHUNK = 16
PLAN_HEAD = 8
MIB = 2**20
SMALL = 2 * MIB
BF16 = jnp.bfloat16
F32 = jnp.float32


def split_parts(value):
    high = value.astype(BF16)
    low = (value - high.astype(F32)).astype(BF16)
    return high, low


def prepare_kernel(b_hbm, o_ref, b_ref, t_ref, sems):
    cells, _, slots = b_hbm.shape
    middle, width = cells // 2, min(128, slots)
    copies = []
    for r in range(middle // CHUNK):
        for side in range(2):
            rows = pl.ds(side * middle + r * CHUNK, CHUNK)
            copies.append(pltpu.make_async_copy(b_hbm.at[rows], b_ref.at[rows], sems.at[2 * r + side]))
    for copy in copies:
        copy.start()
    o_ref[slots] = jnp.zeros(o_ref.shape[1:], BF16)
    for r in range(middle // CHUNK):
        copies[2 * r].wait()
        copies[2 * r + 1].wait()

        def turn(i, carry, r=r):
            for c in range(slots // width):
                first, second = [b_ref[side * middle + r * CHUNK + i, :, pl.ds(c * width, width)] for side in range(2)]
                t_ref[i, pl.ds(c * width, width), :] = jnp.concatenate([first, second], axis=0).T
            return carry

        lax.fori_loop(0, CHUNK, turn, 0, unroll=True)

        def regroup(g, carry, r=r):
            first = pl.multiple_of(g * 8, 8)
            value = jnp.swapaxes(t_ref[:, pl.ds(first, 8), :], 0, 1)
            other = pltpu.roll(value, cells, 2)
            left = lax.broadcasted_iota(jnp.int32, value.shape, 2) < cells
            value_high, other_high = value.astype(BF16).astype(F32), other.astype(BF16).astype(F32)
            upper = jnp.where(left, value_high, other - other_high)
            lower = jnp.where(left, other_high, value - value_high)
            o_ref[pl.ds(first, 8), pl.ds(r * CHUNK, CHUNK), :] = upper.astype(BF16)
            o_ref[pl.ds(first, 8), pl.ds(middle + r * CHUNK, CHUNK), :] = lower.astype(BF16)
            return carry

        lax.fori_loop(0, slots // 8, regroup, 0, unroll=True)


def prepare(blocks):
    slots, cells, _ = blocks.shape
    return pl.pallas_call(
        prepare_kernel,
        in_specs=[pl.BlockSpec(memory_space=pltpu.HBM)],
        out_specs=pl.BlockSpec(memory_space=pltpu.VMEM),
        out_shape=jax.ShapeDtypeStruct((slots + 1, cells, 2 * cells), BF16),
        scratch_shapes=[
            pltpu.VMEM((cells, cells, slots), F32),
            pltpu.VMEM((CHUNK, slots, 2 * cells), F32),
            pltpu.SemaphoreType.DMA((cells // CHUNK,)),
        ],
        compiler_params=pltpu.CompilerParams(vmem_limit_bytes=14 * MIB),
        cost_estimate=pl.CostEstimate(flops=0, bytes_accessed=24 * MIB, transcendentals=0),
        name="prepare",
    )(pltpu.with_memory_space_constraint(jnp.transpose(blocks, (1, 2, 0)), pltpu.HBM))


def transfer_kernel(fields_at, begin, end, has_before, plan_ref, a_ref, *rest):
    x_refs, (out_ref, w_ref) = rest[: len(fields_at)], rest[-2:]
    zero_slot, cells = a_ref.shape[0] - 1, a_ref.shape[1]
    length = (plan_ref.shape[0] - PLAN_HEAD) // 3
    for x_ref, at in zip(x_refs, fields_at):

        def split_brick(c, carry, x_ref=x_ref, at=at):
            w_ref[at + c] = jnp.concatenate(split_parts(x_ref[c]), axis=0)
            return carry

        lax.fori_loop(0, x_ref.shape[0], split_brick, 0, unroll=True)

    def clear(c, carry):
        out_ref[c] = rest[-3][c] if has_before else jnp.zeros(out_ref.shape[1:], F32)
        return carry

    lax.fori_loop(0, out_ref.shape[0], clear, 0, unroll=4)
    first, last = plan_ref[begin], plan_ref[end]

    def step(g, carry, size, first):
        results, targets = [], []
        for u in range(size):
            s = first + g * size + u
            a = a_ref[jnp.where(s < last, plan_ref[PLAN_HEAD + s], zero_slot)]
            w = w_ref[jnp.where(s < last, plan_ref[PLAN_HEAD + 2 * length + s], fields_at[0])]
            targets.append(plan_ref[PLAN_HEAD + length + s])
            high, low = w[:cells], w[cells:]
            results.append(
                jnp.dot(
                    jnp.concatenate([a, a], axis=1),
                    jnp.concatenate([high, high, low, low], axis=0),
                    preferred_element_type=F32,
                )
            )
        for u in range(size):
            out_ref[targets[u]] += results[u]
        return carry

    large = (last - first + GROUP // 2 - 1) // GROUP
    lax.fori_loop(0, large, functools.partial(step, size=GROUP, first=first), 0)
    rest_first = first + large * GROUP
    small = jnp.where(rest_first < last, 1, 0)
    lax.fori_loop(0, small, functools.partial(step, size=GROUP // 2, first=rest_first), 0)


def transfer(plan, matrix, fields, fields_at, senders, begin, end, before, out_bricks):
    cells, lights = fields[0].shape[1:]
    whole = pl.BlockSpec(memory_space=pltpu.VMEM)
    scratch = senders * 2 * cells * lights * 2
    rows = matrix.shape[0] * cells * (end - begin) // STAGES
    return pl.pallas_call(
        functools.partial(transfer_kernel, fields_at, begin, end, len(before)),
        in_specs=[pl.BlockSpec(memory_space=pltpu.SMEM)] + [whole] * (1 + len(fields) + len(before)),
        out_specs=whole,
        out_shape=jax.ShapeDtypeStruct((out_bricks, cells, lights), F32),
        scratch_shapes=[pltpu.VMEM((senders, 2 * cells, lights), BF16)],
        compiler_params=pltpu.CompilerParams(vmem_limit_bytes=SMALL + scratch),
        cost_estimate=pl.CostEstimate(flops=0, bytes_accessed=0, transcendentals=0),
        name="transfer",
    )(pltpu.with_memory_space_constraint(plan, pltpu.SMEM), matrix, *fields, *before)


def keep_kernel(value_ref, out_ref, sem):
    copy = pltpu.make_async_copy(value_ref, out_ref, sem)
    copy.start()
    copy.wait()


def in_scalar_memory(value):
    return pl.pallas_call(
        keep_kernel,
        in_specs=[pl.BlockSpec(memory_space=pltpu.VMEM)],
        out_specs=pl.BlockSpec(memory_space=pltpu.SMEM),
        out_shape=pltpu.SMEM(value.shape, value.dtype),
        scratch_shapes=[pltpu.SemaphoreType.DMA],
        compiler_params=pltpu.CompilerParams(vmem_limit_bytes=SMALL),
        name="keep",
    )(value)


def first_of_line():
    me, n = lax.axis_index("col"), lax.axis_size("col")
    return jnp.where(me % 2 == 0, me == 0, me == n - 1)


def small_call(kernel, out_bricks, name, *args, after=()):
    whole, anywhere = pl.BlockSpec(memory_space=pltpu.VMEM), pl.BlockSpec(memory_space=pl.ANY)
    shape = args[0].shape[1:]
    return pl.pallas_call(
        kernel,
        in_specs=[whole] * len(args) + [anywhere] * len(after),
        out_specs=[whole] * len(out_bricks),
        out_shape=[jax.ShapeDtypeStruct((n, *shape), F32) for n in out_bricks],
        compiler_params=pltpu.CompilerParams(vmem_limit_bytes=SMALL),
        cost_estimate=pl.CostEstimate(flops=0, bytes_accessed=0, transcendentals=0),
        name=name,
    )(*args, *after)


def carry_kernel(mine, other, sums_ref, got_ref, *rest):
    came_refs, out_ref = rest[:-1], rest[-1]
    first = first_of_line()
    for c in range(out_ref.shape[0]):
        total = sums_ref[mine + c] + got_ref[other + c]
        if came_refs:
            total += jnp.where(first, 0.0, came_refs[0][c])
        out_ref[c] = total


def finish_kernel(half_at, owns, skipped, source_ref, sums_ref, *rest):
    out_ref = rest[-1]
    first = first_of_line()
    per = (len(rest) - 1) // len(owns)
    for h, own in enumerate(owns):
        got_ref, *ends = rest[h * per : (h + 1) * per]
        half = out_ref.shape[0] // len(owns)
        for c in range(half):
            total = source_ref[(half_at + h) * half + c] + (sums_ref[own + c] + got_ref[own - skipped + half + c])
            if ends:
                total += jnp.where(first, 0.0, ends[0][c]) + ends[1][c]
            out_ref[h * half + c] = total


def cross_kernel(came_ref, *rest):
    out_ref = rest[-1]
    half, first = out_ref.shape[0], first_of_line()
    for c in range(half):
        out_ref[c] = jnp.where(first, 0.0, came_ref[half + c])


def cut_kernel(at, value_ref, *rest):
    out_ref = rest[-1]
    out_ref[...] = value_ref[at : at + out_ref.shape[0]]


def sums_at(h, distance, pairs, half):
    order = (distance + pairs - 1) % pairs if pairs > 1 else distance
    size = 2 * half
    return jnp.where(order == 0, h * size, (PARTS + h * (pairs - 1) + order - 1) * size)


def make_plan(row_index, col_index, live, bricks, n_row, n_col, flips):
    pairs, half = n_col // 2, bricks // PARTS
    my_row, me = lax.axis_index("row"), lax.axis_index("col")
    my_pair, my_side = me // 2, me % 2
    column, brick = row_index // bricks, row_index % bricks
    pair, side = column // 2, column % 2
    ahead = jnp.where(my_side == 0, pair - my_pair, my_pair - pair) % pairs
    carrier = jnp.where(pair > my_pair, 0, jnp.where(pair < my_pair, 1, my_side))
    place = sums_at(brick // half, ahead, pairs, half) + (side ^ carrier) * half + brick % half

    from_row, from_brick = col_index // bricks, col_index % bricks
    turn = from_row ^ my_row if flips else (from_row - my_row) % n_row
    sender = turn * bricks + from_brick

    n = row_index.shape[0]
    slots = jnp.arange(n, dtype=jnp.int32)
    part = jnp.where(turn == 0, 0, jnp.where(turn < n_row - 1, 1, jnp.where(place < PARTS * 2 * half, 2, 3)))
    part = jnp.where(slots < live, part, STAGES)
    key = part * n + slots
    rank = jnp.sum(key[None, :] < key[:, None], axis=1, dtype=jnp.int32)
    chosen = rank[None, :] == jnp.arange(n + GROUP, dtype=jnp.int32)[:, None]

    def in_order(value):
        return jnp.sum(jnp.where(chosen, value[None, :], 0), axis=1, dtype=jnp.int32)

    bounds = jnp.arange(PLAN_HEAD, dtype=jnp.int32)
    starts = jnp.sum(part[None, :] < bounds[:, None], axis=1, dtype=jnp.int32)
    return jnp.concatenate([starts, in_order(slots), in_order(place), in_order(sender)])


def body(source, blocks, row_index, col_index, live_count):
    bricks = source.shape[0]
    n_row, n_col = lax.axis_size("row"), lax.axis_size("col")
    pairs, half = n_col // 2, bricks // PARTS
    block = 2 * half
    flips = n_row & (n_row - 1) == 0

    swap = [(i, i ^ 1) for i in range(n_col)]
    ring = [(i, (i + 2 if i + 2 < n_col else n_col - 1) if i % 2 == 0 else (i - 2 if i > 2 else 0)) for i in range(n_col)]

    def from_turn(value, k):
        return lax.ppermute(value, "row", [(i ^ k if flips else (i + k) % n_row, i) for i in range(n_row)])

    def gather(values, direct):
        return [[from_turn(v, k) for v in values] for k in range(1, n_row if direct else n_row - 1)]

    def cut(value, at, size, after):
        return small_call(functools.partial(cut_kernel, at), (size,), "cut", value, after=after)[0]

    def forward(value, k, *after):
        return from_turn(cut(value, 0, value.shape[0], after), k)

    def apply(turns, first, end, *before):
        fields = [f for pieces in turns.values() for f in pieces]
        at = [k * bricks + sum(f.shape[0] for f in pieces[:i]) for k, pieces in turns.items() for i in range(len(pieces))]
        return transfer(plan, matrix, fields, at, n_row * bricks, first, end, before, bricks * n_col)

    leading = PARTS * block

    def at(h, distance):
        order = (distance + pairs - 1) % pairs
        return h * block if order == 0 else leading + (h * (pairs - 1) + order - 1) * block

    def scatter(lead, sums):
        first = lax.ppermute(lead[:leading], "col", swap)
        if pairs == 1:
            return [[first]] * PARTS
        far = pairs - 1
        totals = []
        for h in range(PARTS):
            kernel = functools.partial(carry_kernel, at(h, far), h * block)
            totals += small_call(kernel, (block,), "carry", sums, first)
        rest = lax.ppermute(cut(sums, leading, sums.shape[0] - leading, totals), "col", swap)
        parts = []
        for h in range(PARTS):
            came = lax.ppermute(totals[h], "col", ring)
            for distance in range(far - 1, 0, -1):
                kernel = functools.partial(carry_kernel, at(h, distance), at(h, pairs - distance) - leading)
                total = small_call(kernel, (block,), "carry", sums, rest, came)[0]
                came = lax.ppermute(total, "col", ring)
            parts.append([rest, came])
        return parts

    def finish(sums, parts, half_at, after=()):
        args = []
        for rest, *came in parts:
            args += [rest, *came]
            if came:
                crossing = small_call(cross_kernel, (half,), "cross", *came, after=after)[0]
                args.append(lax.ppermute(crossing, "col", swap))
        owns = [at(half_at + h, 0) for h in range(len(parts))]
        kernel = functools.partial(finish_kernel, half_at, owns, leading if pairs > 1 else 0)
        return small_call(kernel, (len(parts) * half,), "finish", source, sums, *args)[0]

    plan = in_scalar_memory(make_plan(row_index, col_index, live_count[0], bricks, n_row, n_col, flips))
    matrix = prepare(blocks)

    def by_row(field):
        return dict(enumerate([field, *gather(field, True)]))

    def last_row(last, sums):
        lead = apply({3: last}, 2, 3, sums)
        return lead, apply({3: last}, 3, STAGES, lead)

    if n_row == 4:
        one, two = gather([source], False)
        last = [forward(one[0][: bricks // 2], 2, matrix), forward(two[0][bricks // 2 :], 1, matrix)]
        lead, sums = last_row(last, apply({0: [source], 1: one, 2: two}, 0, 2))
    else:
        lead = sums = apply(by_row([source]), 0, STAGES)
    for _ in range(ITERS - 1):
        field = []
        parts = scatter(lead, sums)
        for begin, end in GROUPS:
            field.append(finish(sums, parts[begin:end], begin, field))
        if n_row == 4:
            one, two = gather(field, False)
            sums = apply({0: field}, 0, 1)
            last = [forward(one[0], 2), forward(two[1], 1, sums)]
            lead, sums = last_row(last, apply({1: one, 2: two}, 1, 2, sums))
        else:
            lead = sums = apply(by_row(field), 0, STAGES)
    return finish(sums, scatter(lead, sums), 0)


def solution(mesh):
    in_specs = (
        P(("row", "col"), None, None),
        P(("row", "col"), None, None),
        P(("row", "col")),
        P(("row", "col")),
        P(("row", "col")),
    )
    out_specs = P(("row", "col"), None, None)
    return jax.shard_map(body, mesh=mesh, in_specs=in_specs, out_specs=out_specs, check_vma=False)
```

```python
import functools

import jax
import jax.numpy as jnp
from jax import lax
from jax.experimental import pallas as pl
from jax.experimental.pallas import tpu as pltpu
from jax.sharding import PartitionSpec as P

ITERS = 2
PARTS = 4
GROUPS = (0, 2), (2, 4)
STAGES = 4
GROUP = 32
CHUNK = 16
PLAN_HEAD = 8
MIB = 2**20
SMALL = 2 * MIB
BF16 = jnp.bfloat16
F32 = jnp.float32


def split_parts(value):
    high = value.astype(BF16)
    low = (value - high.astype(F32)).astype(BF16)
    return high, low


def prepare_kernel(b_hbm, o_ref, b_ref, t_ref, sems):
    cells, _, slots = b_hbm.shape
    middle, width = cells // 2, min(128, slots)
    copies = []
    for r in range(middle // CHUNK):
        for side in range(2):
            rows = pl.ds(side * middle + r * CHUNK, CHUNK)
            copies.append(pltpu.make_async_copy(b_hbm.at[rows], b_ref.at[rows], sems.at[2 * r + side]))
    for copy in copies:
        copy.start()
    o_ref[slots] = jnp.zeros(o_ref.shape[1:], BF16)
    for r in range(middle // CHUNK):
        copies[2 * r].wait()
        copies[2 * r + 1].wait()

        def turn(i, carry, r=r):
            for c in range(slots // width):
                first, second = [b_ref[side * middle + r * CHUNK + i, :, pl.ds(c * width, width)] for side in range(2)]
                t_ref[i, pl.ds(c * width, width), :] = jnp.concatenate([first, second], axis=0).T
            return carry

        lax.fori_loop(0, CHUNK, turn, 0, unroll=True)

        def regroup(g, carry, r=r):
            first = pl.multiple_of(g * 8, 8)
            value = jnp.swapaxes(t_ref[:, pl.ds(first, 8), :], 0, 1)
            other = pltpu.roll(value, cells, 2)
            left = lax.broadcasted_iota(jnp.int32, value.shape, 2) < cells
            value_high, other_high = value.astype(BF16).astype(F32), other.astype(BF16).astype(F32)
            upper = jnp.where(left, value_high, other - other_high)
            lower = jnp.where(left, other_high, value - value_high)
            o_ref[pl.ds(first, 8), pl.ds(r * CHUNK, CHUNK), :] = upper.astype(BF16)
            o_ref[pl.ds(first, 8), pl.ds(middle + r * CHUNK, CHUNK), :] = lower.astype(BF16)
            return carry

        lax.fori_loop(0, slots // 8, regroup, 0, unroll=True)


def prepare(blocks):
    slots, cells, _ = blocks.shape
    return pl.pallas_call(
        prepare_kernel,
        in_specs=[pl.BlockSpec(memory_space=pltpu.HBM)],
        out_specs=pl.BlockSpec(memory_space=pltpu.VMEM),
        out_shape=jax.ShapeDtypeStruct((slots + 1, cells, 2 * cells), BF16),
        scratch_shapes=[
            pltpu.VMEM((cells, cells, slots), F32),
            pltpu.VMEM((CHUNK, slots, 2 * cells), F32),
            pltpu.SemaphoreType.DMA((cells // CHUNK,)),
        ],
        compiler_params=pltpu.CompilerParams(vmem_limit_bytes=14 * MIB),
        cost_estimate=pl.CostEstimate(flops=0, bytes_accessed=24 * MIB, transcendentals=0),
        name="prepare",
    )(pltpu.with_memory_space_constraint(jnp.transpose(blocks, (1, 2, 0)), pltpu.HBM))


def transfer_kernel(fields_at, begin, end, has_before, plan_ref, a_ref, *rest):
    x_refs, (out_ref, w_ref) = rest[: len(fields_at)], rest[-2:]
    zero_slot, cells = a_ref.shape[0] - 1, a_ref.shape[1]
    length = (plan_ref.shape[0] - PLAN_HEAD) // 3
    for x_ref, at in zip(x_refs, fields_at):

        def split_brick(c, carry, x_ref=x_ref, at=at):
            w_ref[at + c] = jnp.concatenate(split_parts(x_ref[c]), axis=0)
            return carry

        lax.fori_loop(0, x_ref.shape[0], split_brick, 0, unroll=True)

    def clear(c, carry):
        out_ref[c] = rest[-3][c] if has_before else jnp.zeros(out_ref.shape[1:], F32)
        return carry

    lax.fori_loop(0, out_ref.shape[0], clear, 0, unroll=4)
    first, last = plan_ref[begin], plan_ref[end]

    def step(g, carry, size, first):
        results, targets = [], []
        for u in range(size):
            s = first + g * size + u
            a = a_ref[jnp.where(s < last, plan_ref[PLAN_HEAD + s], zero_slot)]
            w = w_ref[jnp.where(s < last, plan_ref[PLAN_HEAD + 2 * length + s], fields_at[0])]
            targets.append(plan_ref[PLAN_HEAD + length + s])
            high, low = w[:cells], w[cells:]
            results.append(
                jnp.dot(
                    jnp.concatenate([a, a], axis=1),
                    jnp.concatenate([high, high, low, low], axis=0),
                    preferred_element_type=F32,
                )
            )
        for u in range(size):
            out_ref[targets[u]] += results[u]
        return carry

    large = (last - first + GROUP // 2 - 1) // GROUP
    lax.fori_loop(0, large, functools.partial(step, size=GROUP, first=first), 0)
    rest_first = first + large * GROUP
    small = jnp.where(rest_first < last, 1, 0)
    lax.fori_loop(0, small, functools.partial(step, size=GROUP // 2, first=rest_first), 0)


def transfer(plan, matrix, fields, fields_at, senders, begin, end, before, out_bricks):
    cells, lights = fields[0].shape[1:]
    whole = pl.BlockSpec(memory_space=pltpu.VMEM)
    scratch = senders * 2 * cells * lights * 2
    rows = matrix.shape[0] * cells * (end - begin) // STAGES
    return pl.pallas_call(
        functools.partial(transfer_kernel, fields_at, begin, end, len(before)),
        in_specs=[pl.BlockSpec(memory_space=pltpu.SMEM)] + [whole] * (1 + len(fields) + len(before)),
        out_specs=whole,
        out_shape=jax.ShapeDtypeStruct((out_bricks, cells, lights), F32),
        scratch_shapes=[pltpu.VMEM((senders, 2 * cells, lights), BF16)],
        compiler_params=pltpu.CompilerParams(vmem_limit_bytes=SMALL + scratch),
        cost_estimate=pl.CostEstimate(flops=0, bytes_accessed=0, transcendentals=0),
        name="transfer",
    )(pltpu.with_memory_space_constraint(plan, pltpu.SMEM), matrix, *fields, *before)


def keep_kernel(value_ref, out_ref, sem):
    copy = pltpu.make_async_copy(value_ref, out_ref, sem)
    copy.start()
    copy.wait()


def in_scalar_memory(value):
    return pl.pallas_call(
        keep_kernel,
        in_specs=[pl.BlockSpec(memory_space=pltpu.VMEM)],
        out_specs=pl.BlockSpec(memory_space=pltpu.SMEM),
        out_shape=pltpu.SMEM(value.shape, value.dtype),
        scratch_shapes=[pltpu.SemaphoreType.DMA],
        compiler_params=pltpu.CompilerParams(vmem_limit_bytes=SMALL),
        name="keep",
    )(value)


def first_of_line():
    me, n = lax.axis_index("col"), lax.axis_size("col")
    return jnp.where(me % 2 == 0, me == 0, me == n - 1)


def small_call(kernel, out_bricks, name, *args, after=()):
    whole, anywhere = pl.BlockSpec(memory_space=pltpu.VMEM), pl.BlockSpec(memory_space=pl.ANY)
    shape = args[0].shape[1:]
    return pl.pallas_call(
        kernel,
        in_specs=[whole] * len(args) + [anywhere] * len(after),
        out_specs=[whole] * len(out_bricks),
        out_shape=[jax.ShapeDtypeStruct((n, *shape), F32) for n in out_bricks],
        compiler_params=pltpu.CompilerParams(vmem_limit_bytes=SMALL),
        cost_estimate=pl.CostEstimate(flops=0, bytes_accessed=0, transcendentals=0),
        name=name,
    )(*args, *after)


def carry_kernel(mine, other, sums_ref, got_ref, *rest):
    came_refs, out_ref = rest[:-1], rest[-1]
    first = first_of_line()
    for c in range(out_ref.shape[0]):
        total = sums_ref[mine + c] + got_ref[other + c]
        if came_refs:
            total += jnp.where(first, 0.0, came_refs[0][c])
        out_ref[c] = total


def finish_kernel(half_at, owns, skipped, source_ref, sums_ref, *rest):
    out_ref = rest[-1]
    first = first_of_line()
    per = (len(rest) - 1) // len(owns)
    for h, own in enumerate(owns):
        got_ref, *ends = rest[h * per : (h + 1) * per]
        half = out_ref.shape[0] // len(owns)
        for c in range(half):
            total = source_ref[(half_at + h) * half + c] + (sums_ref[own + c] + got_ref[own - skipped + half + c])
            if ends:
                total += jnp.where(first, 0.0, ends[0][c]) + ends[1][c]
            out_ref[h * half + c] = total


def cross_kernel(came_ref, *rest):
    out_ref = rest[-1]
    half, first = out_ref.shape[0], first_of_line()
    for c in range(half):
        out_ref[c] = jnp.where(first, 0.0, came_ref[half + c])


def cut_kernel(at, value_ref, *rest):
    out_ref = rest[-1]
    out_ref[...] = value_ref[at : at + out_ref.shape[0]]


def sums_at(h, distance, pairs, half):
    order = (distance + pairs - 1) % pairs if pairs > 1 else distance
    size = 2 * half
    return jnp.where(order == 0, h * size, (PARTS + h * (pairs - 1) + order - 1) * size)


def make_plan(row_index, col_index, live, bricks, n_row, n_col, flips):
    pairs, half = n_col // 2, bricks // PARTS
    my_row, me = lax.axis_index("row"), lax.axis_index("col")
    my_pair, my_side = me // 2, me % 2
    column, brick = row_index // bricks, row_index % bricks
    pair, side = column // 2, column % 2
    ahead = jnp.where(my_side == 0, pair - my_pair, my_pair - pair) % pairs
    carrier = jnp.where(pair > my_pair, 0, jnp.where(pair < my_pair, 1, my_side))
    place = sums_at(brick // half, ahead, pairs, half) + (side ^ carrier) * half + brick % half

    from_row, from_brick = col_index // bricks, col_index % bricks
    turn = from_row ^ my_row if flips else (from_row - my_row) % n_row
    sender = turn * bricks + from_brick

    n = row_index.shape[0]
    slots = jnp.arange(n, dtype=jnp.int32)
    part = jnp.where(turn == 0, 0, jnp.where(turn < n_row - 1, 1, jnp.where(place < PARTS * 2 * half, 2, 3)))
    part = jnp.where(slots < live, part, STAGES)
    key = part * n + slots
    rank = jnp.sum(key[None, :] < key[:, None], axis=1, dtype=jnp.int32)
    chosen = rank[None, :] == jnp.arange(n + GROUP, dtype=jnp.int32)[:, None]

    def in_order(value):
        return jnp.sum(jnp.where(chosen, value[None, :], 0), axis=1, dtype=jnp.int32)

    bounds = jnp.arange(PLAN_HEAD, dtype=jnp.int32)
    starts = jnp.sum(part[None, :] < bounds[:, None], axis=1, dtype=jnp.int32)
    return jnp.concatenate([starts, in_order(slots), in_order(place), in_order(sender)])


def body(source, blocks, row_index, col_index, live_count):
    bricks = source.shape[0]
    n_row, n_col = lax.axis_size("row"), lax.axis_size("col")
    pairs, half = n_col // 2, bricks // PARTS
    block = 2 * half
    flips = n_row & (n_row - 1) == 0

    swap = [(i, i ^ 1) for i in range(n_col)]
    ring = [(i, (i + 2 if i + 2 < n_col else n_col - 1) if i % 2 == 0 else (i - 2 if i > 2 else 0)) for i in range(n_col)]

    squares = [(i, (i ^ 2) if (i // 2 + i) % 2 == 0 else i ^ 1) for i in range(n_col)] if pairs % 2 == 0 else ring

    def from_turn(value, k):
        return lax.ppermute(value, "row", [(i ^ k if flips else (i + k) % n_row, i) for i in range(n_row)])

    def gather(values, direct):
        return [[from_turn(v, k) for v in values] for k in range(1, n_row if direct else n_row - 1)]

    def cut(value, at, size, after):
        return small_call(functools.partial(cut_kernel, at), (size,), "cut", value, after=after)[0]

    def forward(value, k, *after):
        return from_turn(cut(value, 0, value.shape[0], after), k)

    def apply(turns, first, end, *before):
        fields = [f for pieces in turns.values() for f in pieces]
        at = [k * bricks + sum(f.shape[0] for f in pieces[:i]) for k, pieces in turns.items() for i in range(len(pieces))]
        return transfer(plan, matrix, fields, at, n_row * bricks, first, end, before, bricks * n_col)

    leading = PARTS * block

    def at(h, distance):
        order = (distance + pairs - 1) % pairs
        return h * block if order == 0 else leading + (h * (pairs - 1) + order - 1) * block

    def scatter(lead, sums):
        first = lax.ppermute(lead[:leading], "col", swap)
        if pairs == 1:
            return [[first]] * PARTS
        far = pairs - 1
        totals = []
        for h in range(PARTS):
            kernel = functools.partial(carry_kernel, at(h, far), h * block)
            totals += small_call(kernel, (block,), "carry", sums, first)
        rest = lax.ppermute(cut(sums, leading, sums.shape[0] - leading, totals), "col", swap)
        parts = []
        for h in range(PARTS):
            came = lax.ppermute(totals[h], "col", squares)
            for distance in range(far - 1, 0, -1):
                kernel = functools.partial(carry_kernel, at(h, distance), at(h, pairs - distance) - leading)
                total = small_call(kernel, (block,), "carry", sums, rest, came)[0]
                came = lax.ppermute(total, "col", ring)
            parts.append([rest, came])
        return parts

    def finish(sums, parts, half_at, after=()):
        args = []
        for rest, *came in parts:
            args += [rest, *came]
            if came:
                crossing = small_call(cross_kernel, (half,), "cross", *came, after=after)[0]
                args.append(lax.ppermute(crossing, "col", swap))
        owns = [at(half_at + h, 0) for h in range(len(parts))]
        kernel = functools.partial(finish_kernel, half_at, owns, leading if pairs > 1 else 0)
        return small_call(kernel, (len(parts) * half,), "finish", source, sums, *args)[0]

    plan = in_scalar_memory(make_plan(row_index, col_index, live_count[0], bricks, n_row, n_col, flips))
    matrix = prepare(blocks)

    def by_row(field):
        return dict(enumerate([field, *gather(field, True)]))

    def last_row(last, sums):
        lead = apply({3: last}, 2, 3, sums)
        return lead, apply({3: last}, 3, STAGES, lead)

    if n_row == 4:
        one, two = gather([source], False)
        last = [forward(one[0][: bricks // 2], 2, matrix), forward(two[0][bricks // 2 :], 1, matrix)]
        lead, sums = last_row(last, apply({0: [source], 1: one, 2: two}, 0, 2))
    else:
        lead = sums = apply(by_row([source]), 0, STAGES)
    for _ in range(ITERS - 1):
        field = []
        parts = scatter(lead, sums)
        for begin, end in GROUPS:
            field.append(finish(sums, parts[begin:end], begin, field))
        if n_row == 4:
            one, two = gather(field, False)
            sums = apply({0: field}, 0, 1)
            last = [forward(one[0], 2), forward(two[1], 1, sums)]
            lead, sums = last_row(last, apply({1: one, 2: two}, 1, 2, sums))
        else:
            lead = sums = apply(by_row(field), 0, STAGES)
    return finish(sums, scatter(lead, sums), 0)


def solution(mesh):
    in_specs = (
        P(("row", "col"), None, None),
        P(("row", "col"), None, None),
        P(("row", "col")),
        P(("row", "col")),
        P(("row", "col")),
    )
    out_specs = P(("row", "col"), None, None)
    return jax.shard_map(body, mesh=mesh, in_specs=in_specs, out_specs=out_specs, check_vma=False)
```

```python
import functools

import jax
import jax.numpy as jnp
from jax import lax
from jax.experimental import pallas as pl
from jax.experimental.pallas import tpu as pltpu
from jax.sharding import PartitionSpec as P

ITERS = 2
PARTS = 4
GROUPS = (0, 2), (2, 4)
STAGES = 4
GROUP = 32
CHUNK = 16
PLAN_HEAD = 8
MIB = 2**20
SMALL = 2 * MIB
BF16 = jnp.bfloat16
F32 = jnp.float32


def split_parts(value):
    high = value.astype(BF16)
    low = (value - high.astype(F32)).astype(BF16)
    return high, low


def prepare_kernel(b_hbm, o_ref, b_ref, t_ref, sems):
    cells, _, slots = b_hbm.shape
    middle, width = cells // 2, min(128, slots)
    copies = []
    for r in range(middle // CHUNK):
        for side in range(2):
            rows = pl.ds(side * middle + r * CHUNK, CHUNK)
            copies.append(pltpu.make_async_copy(b_hbm.at[rows], b_ref.at[rows], sems.at[2 * r + side]))
    for copy in copies:
        copy.start()
    o_ref[slots] = jnp.zeros(o_ref.shape[1:], BF16)
    for r in range(middle // CHUNK):
        copies[2 * r].wait()
        copies[2 * r + 1].wait()

        def turn(i, carry, r=r):
            for c in range(slots // width):
                first, second = [b_ref[side * middle + r * CHUNK + i, :, pl.ds(c * width, width)] for side in range(2)]
                t_ref[i, pl.ds(c * width, width), :] = jnp.concatenate([first, second], axis=0).T
            return carry

        lax.fori_loop(0, CHUNK, turn, 0, unroll=True)

        def regroup(g, carry, r=r):
            first = pl.multiple_of(g * 8, 8)
            value = jnp.swapaxes(t_ref[:, pl.ds(first, 8), :], 0, 1)
            other = pltpu.roll(value, cells, 2)
            left = lax.broadcasted_iota(jnp.int32, value.shape, 2) < cells
            value_high, other_high = value.astype(BF16).astype(F32), other.astype(BF16).astype(F32)
            upper = jnp.where(left, value_high, other - other_high)
            lower = jnp.where(left, other_high, value - value_high)
            o_ref[pl.ds(first, 8), pl.ds(r * CHUNK, CHUNK), :] = upper.astype(BF16)
            o_ref[pl.ds(first, 8), pl.ds(middle + r * CHUNK, CHUNK), :] = lower.astype(BF16)
            return carry

        lax.fori_loop(0, slots // 8, regroup, 0, unroll=True)


def prepare(blocks):
    slots, cells, _ = blocks.shape
    return pl.pallas_call(
        prepare_kernel,
        in_specs=[pl.BlockSpec(memory_space=pltpu.HBM)],
        out_specs=pl.BlockSpec(memory_space=pltpu.VMEM),
        out_shape=jax.ShapeDtypeStruct((slots + 1, cells, 2 * cells), BF16),
        scratch_shapes=[
            pltpu.VMEM((cells, cells, slots), F32),
            pltpu.VMEM((CHUNK, slots, 2 * cells), F32),
            pltpu.SemaphoreType.DMA((cells // CHUNK,)),
        ],
        compiler_params=pltpu.CompilerParams(vmem_limit_bytes=14 * MIB),
        cost_estimate=pl.CostEstimate(flops=0, bytes_accessed=24 * MIB, transcendentals=0),
        name="prepare",
    )(pltpu.with_memory_space_constraint(jnp.transpose(blocks, (1, 2, 0)), pltpu.HBM))


def transfer_kernel(fields_at, begin, end, has_before, plan_ref, a_ref, *rest):
    x_refs, (out_ref, w_ref) = rest[: len(fields_at)], rest[-2:]
    zero_slot, cells = a_ref.shape[0] - 1, a_ref.shape[1]
    length = (plan_ref.shape[0] - PLAN_HEAD) // 3
    for x_ref, at in zip(x_refs, fields_at):

        def split_brick(c, carry, x_ref=x_ref, at=at):
            w_ref[at + c] = jnp.concatenate(split_parts(x_ref[c]), axis=0)
            return carry

        lax.fori_loop(0, x_ref.shape[0], split_brick, 0, unroll=True)

    def clear(c, carry):
        out_ref[c] = rest[-3][c] if has_before else jnp.zeros(out_ref.shape[1:], F32)
        return carry

    lax.fori_loop(0, out_ref.shape[0], clear, 0, unroll=4)
    first, last = plan_ref[begin], plan_ref[end]

    def step(g, carry, size, first):
        results, targets = [], []
        for u in range(size):
            s = first + g * size + u
            a = a_ref[jnp.where(s < last, plan_ref[PLAN_HEAD + s], zero_slot)]
            w = w_ref[jnp.where(s < last, plan_ref[PLAN_HEAD + 2 * length + s], fields_at[0])]
            targets.append(plan_ref[PLAN_HEAD + length + s])
            high, low = w[:cells], w[cells:]
            results.append(
                jnp.dot(
                    jnp.concatenate([a, a], axis=1),
                    jnp.concatenate([high, high, low, low], axis=0),
                    preferred_element_type=F32,
                )
            )
        for u in range(size):
            out_ref[targets[u]] += results[u]
        return carry

    huge = (last - first) // (2 * GROUP)
    lax.fori_loop(0, huge, functools.partial(step, size=2 * GROUP, first=first), 0)
    first += huge * 2 * GROUP
    large = (last - first + GROUP // 2 - 1) // GROUP
    lax.fori_loop(0, large, functools.partial(step, size=GROUP, first=first), 0)
    rest_first = first + large * GROUP
    small = jnp.where(rest_first < last, 1, 0)
    lax.fori_loop(0, small, functools.partial(step, size=GROUP // 2, first=rest_first), 0)


def transfer(plan, matrix, fields, fields_at, senders, begin, end, before, out_bricks):
    cells, lights = fields[0].shape[1:]
    whole = pl.BlockSpec(memory_space=pltpu.VMEM)
    scratch = senders * 2 * cells * lights * 2
    rows = matrix.shape[0] * cells * (end - begin) // STAGES
    return pl.pallas_call(
        functools.partial(transfer_kernel, fields_at, begin, end, len(before)),
        in_specs=[pl.BlockSpec(memory_space=pltpu.SMEM)] + [whole] * (1 + len(fields) + len(before)),
        out_specs=whole,
        out_shape=jax.ShapeDtypeStruct((out_bricks, cells, lights), F32),
        scratch_shapes=[pltpu.VMEM((senders, 2 * cells, lights), BF16)],
        compiler_params=pltpu.CompilerParams(vmem_limit_bytes=SMALL + scratch),
        cost_estimate=pl.CostEstimate(flops=0, bytes_accessed=0, transcendentals=0),
        name="transfer",
    )(pltpu.with_memory_space_constraint(plan, pltpu.SMEM), matrix, *fields, *before)


def keep_kernel(value_ref, out_ref, sem):
    copy = pltpu.make_async_copy(value_ref, out_ref, sem)
    copy.start()
    copy.wait()


def in_scalar_memory(value):
    return pl.pallas_call(
        keep_kernel,
        in_specs=[pl.BlockSpec(memory_space=pltpu.VMEM)],
        out_specs=pl.BlockSpec(memory_space=pltpu.SMEM),
        out_shape=pltpu.SMEM(value.shape, value.dtype),
        scratch_shapes=[pltpu.SemaphoreType.DMA],
        compiler_params=pltpu.CompilerParams(vmem_limit_bytes=SMALL),
        name="keep",
    )(value)


def first_of_line():
    me, n = lax.axis_index("col"), lax.axis_size("col")
    return jnp.where(me & 1 == 0, me == 0, me == n - 1)


def small_call(kernel, out_bricks, name, *args, after=()):
    whole, anywhere = pl.BlockSpec(memory_space=pltpu.VMEM), pl.BlockSpec(memory_space=pl.ANY)
    shape = args[0].shape[1:]
    return pl.pallas_call(
        kernel,
        in_specs=[whole] * len(args) + [anywhere] * len(after),
        out_specs=[whole] * len(out_bricks),
        out_shape=[jax.ShapeDtypeStruct((n, *shape), F32) for n in out_bricks],
        compiler_params=pltpu.CompilerParams(vmem_limit_bytes=SMALL),
        cost_estimate=pl.CostEstimate(flops=0, bytes_accessed=0, transcendentals=0),
        name=name,
    )(*args, *after)


def carry_kernel(mine, other, sums_ref, got_ref, *rest):
    came_refs, out_ref = rest[:-1], rest[-1]
    first = first_of_line()
    for c in range(out_ref.shape[0]):
        total = sums_ref[mine + c] + got_ref[other + c]
        if came_refs:
            total += jnp.where(first, 0.0, came_refs[0][c])
        out_ref[c] = total


def finish_kernel(half_at, owns, skipped, source_ref, sums_ref, *rest):
    out_ref = rest[-1]
    first = first_of_line()
    per = (len(rest) - 1) // len(owns)
    for h, own in enumerate(owns):
        got_ref, *ends = rest[h * per : (h + 1) * per]
        half = out_ref.shape[0] // len(owns)
        for c in range(half):
            total = source_ref[(half_at + h) * half + c] + (sums_ref[own + c] + got_ref[own - skipped + half + c])
            if ends:
                total += jnp.where(first, 0.0, ends[0][c]) + ends[1][c]
            out_ref[h * half + c] = total


def cross_kernel(came_ref, *rest):
    out_ref = rest[-1]
    half, first = out_ref.shape[0], first_of_line()
    for c in range(half):
        out_ref[c] = jnp.where(first, 0.0, came_ref[half + c])


def cut_kernel(at, value_ref, *rest):
    out_ref = rest[-1]
    out_ref[...] = value_ref[at : at + out_ref.shape[0]]


def sums_at(h, distance, pairs, half):
    order = lax.rem(distance + pairs - 1, pairs) if pairs > 1 else distance
    size = 2 * half
    return jnp.where(order == 0, h * size, (PARTS + h * (pairs - 1) + order - 1) * size)


def make_plan(row_index, col_index, live, bricks, n_row, n_col, flips):
    pairs, half = n_col // 2, bricks // PARTS
    my_row, me = lax.axis_index("row"), lax.axis_index("col")
    my_pair, my_side = me >> 1, me & 1
    column, brick = lax.div(row_index, bricks), lax.rem(row_index, bricks)
    pair, side = column >> 1, column & 1
    ahead = lax.rem(jnp.where(my_side == 0, pair - my_pair, my_pair - pair) + pairs, pairs)
    carrier = jnp.where(pair > my_pair, 0, jnp.where(pair < my_pair, 1, my_side))
    place = sums_at(lax.div(brick, half), ahead, pairs, half) + (side ^ carrier) * half + lax.rem(brick, half)

    from_row, from_brick = lax.div(col_index, bricks), lax.rem(col_index, bricks)
    turn = from_row ^ my_row if flips else lax.rem(from_row - my_row + n_row, n_row)
    sender = turn * bricks + from_brick

    n = row_index.shape[0]
    slots = jnp.arange(n, dtype=jnp.int32)
    part = jnp.where(turn == 0, 0, jnp.where(turn < n_row - 1, 1, jnp.where(place < PARTS * 2 * half, 2, 3)))
    part = jnp.where(slots < live, part, STAGES)
    key = part * n + slots
    rank = jnp.sum(key[None, :] < key[:, None], axis=1, dtype=jnp.int32)
    chosen = rank[None, :] == jnp.arange(n + GROUP, dtype=jnp.int32)[:, None]

    def in_order(value):
        return jnp.sum(jnp.where(chosen, value[None, :], 0), axis=1, dtype=jnp.int32)

    bounds = jnp.arange(PLAN_HEAD, dtype=jnp.int32)
    starts = jnp.sum(part[None, :] < bounds[:, None], axis=1, dtype=jnp.int32)
    return jnp.concatenate([starts, in_order(slots), in_order(place), in_order(sender)])


def body(source, blocks, row_index, col_index, live_count):
    bricks = source.shape[0]
    n_row, n_col = lax.axis_size("row"), lax.axis_size("col")
    pairs, half = n_col // 2, bricks // PARTS
    block = 2 * half
    flips = n_row & (n_row - 1) == 0

    swap = [(i, i ^ 1) for i in range(n_col)]
    ring = [(i, (i + 2 if i + 2 < n_col else n_col - 1) if i % 2 == 0 else (i - 2 if i > 2 else 0)) for i in range(n_col)]

    squares = [(i, (i ^ 2) if (i // 2 + i) % 2 == 0 else i ^ 1) for i in range(n_col)] if pairs % 2 == 0 else ring

    def from_turn(value, k):
        return lax.ppermute(value, "row", [(i ^ k if flips else (i + k) % n_row, i) for i in range(n_row)])

    def gather(values, direct):
        return [[from_turn(v, k) for v in values] for k in range(1, n_row if direct else n_row - 1)]

    def cut(value, at, size, after):
        return small_call(functools.partial(cut_kernel, at), (size,), "cut", value, after=after)[0]

    def forward(value, k, *after):
        return from_turn(cut(value, 0, value.shape[0], after), k)

    def apply(turns, first, end, *before):
        fields = [f for pieces in turns.values() for f in pieces]
        at = [k * bricks + sum(f.shape[0] for f in pieces[:i]) for k, pieces in turns.items() for i in range(len(pieces))]
        return transfer(plan, matrix, fields, at, n_row * bricks, first, end, before, bricks * n_col)

    leading = PARTS * block

    def at(h, distance):
        order = (distance + pairs - 1) % pairs
        return h * block if order == 0 else leading + (h * (pairs - 1) + order - 1) * block

    def scatter(lead, sums):
        first = lax.ppermute(lead[:leading], "col", swap)
        if pairs == 1:
            return [[first]] * PARTS
        far = pairs - 1
        totals = []
        for h in range(PARTS):
            kernel = functools.partial(carry_kernel, at(h, far), h * block)
            totals += small_call(kernel, (block,), "carry", sums, first)
        rest = lax.ppermute(cut(sums, leading, sums.shape[0] - leading, totals), "col", swap)
        parts = []
        for h in range(PARTS):
            came = lax.ppermute(totals[h], "col", squares)
            for distance in range(far - 1, 0, -1):
                kernel = functools.partial(carry_kernel, at(h, distance), at(h, pairs - distance) - leading)
                total = small_call(kernel, (block,), "carry", sums, rest, came)[0]
                came = lax.ppermute(total, "col", ring)
            parts.append([rest, came])
        return parts

    def finish(sums, parts, half_at, after=()):
        args = []
        for rest, *came in parts:
            args += [rest, *came]
            if came:
                crossing = small_call(cross_kernel, (half,), "cross", *came, after=after)[0]
                args.append(lax.ppermute(crossing, "col", swap))
        owns = [at(half_at + h, 0) for h in range(len(parts))]
        kernel = functools.partial(finish_kernel, half_at, owns, leading if pairs > 1 else 0)
        return small_call(kernel, (len(parts) * half,), "finish", source, sums, *args)[0]

    plan = in_scalar_memory(make_plan(row_index, col_index, live_count[0], bricks, n_row, n_col, flips))
    matrix = prepare(blocks)

    def by_row(field):
        return dict(enumerate([field, *gather(field, True)]))

    def last_row(last, sums):
        lead = apply({3: last}, 2, 3, sums)
        return lead, apply({3: last}, 3, STAGES, lead)

    if n_row == 4:
        one, two = gather([source], False)
        last = [forward(one[0][: bricks // 2], 2, matrix), forward(two[0][bricks // 2 :], 1, matrix)]
        lead, sums = last_row(last, apply({0: [source], 1: one, 2: two}, 0, 2))
    else:
        lead = sums = apply(by_row([source]), 0, STAGES)
    for _ in range(ITERS - 1):
        field = []
        parts = scatter(lead, sums)
        for begin, end in GROUPS:
            field.append(finish(sums, parts[begin:end], begin, field))
        if n_row == 4:
            one, two = gather(field, False)
            sums = apply({0: field}, 0, 1)
            last = [forward(one[0], 2), forward(two[1], 1, sums)]
            lead, sums = last_row(last, apply({1: one, 2: two}, 1, 2, sums))
        else:
            lead = sums = apply(by_row(field), 0, STAGES)
    return finish(sums, scatter(lead, sums), 0)


def solution(mesh):
    in_specs = (
        P(("row", "col"), None, None),
        P(("row", "col"), None, None),
        P(("row", "col")),
        P(("row", "col")),
        P(("row", "col")),
    )
    out_specs = P(("row", "col"), None, None)
    return jax.shard_map(body, mesh=mesh, in_specs=in_specs, out_specs=out_specs, check_vma=False)
```

```python
import functools

import jax
import jax.numpy as jnp
from jax import lax
from jax.experimental import pallas as pl
from jax.experimental.pallas import tpu as pltpu
from jax.sharding import PartitionSpec as P

ITERS = 2
PARTS = 4
GROUPS = (0, 2), (2, 4)
STAGES = 4
LEADS = 2
GROUP = 32
CHUNK = 16
PLAN_HEAD = 8
MIB = 2**20
SMALL = 2 * MIB
BF16 = jnp.bfloat16
F32 = jnp.float32


def split_parts(value):
    high = value.astype(BF16)
    low = (value - high.astype(F32)).astype(BF16)
    return high, low


def prepare_kernel(b_hbm, o_ref, b_ref, t_ref, sems):
    cells, _, slots = b_hbm.shape
    middle, width = cells // 2, min(128, slots)
    copies = []
    for r in range(middle // CHUNK):
        for side in range(2):
            rows = pl.ds(side * middle + r * CHUNK, CHUNK)
            copies.append(pltpu.make_async_copy(b_hbm.at[rows], b_ref.at[rows], sems.at[2 * r + side]))
    for copy in copies:
        copy.start()
    o_ref[slots] = jnp.zeros(o_ref.shape[1:], BF16)
    for r in range(middle // CHUNK):
        copies[2 * r].wait()
        copies[2 * r + 1].wait()

        def turn(i, carry, r=r):
            for c in range(slots // width):
                first, second = [b_ref[side * middle + r * CHUNK + i, :, pl.ds(c * width, width)] for side in range(2)]
                t_ref[i, pl.ds(c * width, width), :] = jnp.concatenate([first, second], axis=0).T
            return carry

        lax.fori_loop(0, CHUNK, turn, 0, unroll=True)

        def regroup(g, carry, r=r):
            first = pl.multiple_of(g * 8, 8)
            value = jnp.swapaxes(t_ref[:, pl.ds(first, 8), :], 0, 1)
            other = pltpu.roll(value, cells, 2)
            left = lax.broadcasted_iota(jnp.int32, value.shape, 2) < cells
            value_high, other_high = value.astype(BF16).astype(F32), other.astype(BF16).astype(F32)
            upper = jnp.where(left, value_high, other - other_high)
            lower = jnp.where(left, other_high, value - value_high)
            o_ref[pl.ds(first, 8), pl.ds(r * CHUNK, CHUNK), :] = upper.astype(BF16)
            o_ref[pl.ds(first, 8), pl.ds(middle + r * CHUNK, CHUNK), :] = lower.astype(BF16)
            return carry

        lax.fori_loop(0, slots // 8, regroup, 0, unroll=True)


def prepare(blocks):
    slots, cells, _ = blocks.shape
    return pl.pallas_call(
        prepare_kernel,
        in_specs=[pl.BlockSpec(memory_space=pltpu.HBM)],
        out_specs=pl.BlockSpec(memory_space=pltpu.VMEM),
        out_shape=jax.ShapeDtypeStruct((slots + 1, cells, 2 * cells), BF16),
        scratch_shapes=[
            pltpu.VMEM((cells, cells, slots), F32),
            pltpu.VMEM((CHUNK, slots, 2 * cells), F32),
            pltpu.SemaphoreType.DMA((cells // CHUNK,)),
        ],
        compiler_params=pltpu.CompilerParams(vmem_limit_bytes=14 * MIB),
        cost_estimate=pl.CostEstimate(flops=0, bytes_accessed=24 * MIB, transcendentals=0),
        name="prepare",
    )(pltpu.with_memory_space_constraint(jnp.transpose(blocks, (1, 2, 0)), pltpu.HBM))


def transfer_kernel(fields_at, begin, end, has_before, plan_ref, a_ref, *rest):
    x_refs, (out_ref, w_ref) = rest[: len(fields_at)], rest[-2:]
    zero_slot, cells = a_ref.shape[0] - 1, a_ref.shape[1]
    length = (plan_ref.shape[0] - PLAN_HEAD) // 3
    for x_ref, at in zip(x_refs, fields_at):

        def split_brick(c, carry, x_ref=x_ref, at=at):
            w_ref[at + c] = jnp.concatenate(split_parts(x_ref[c]), axis=0)
            return carry

        lax.fori_loop(0, x_ref.shape[0], split_brick, 0, unroll=True)

    def clear(c, carry):
        out_ref[c] = rest[-3][c] if has_before else jnp.zeros(out_ref.shape[1:], F32)
        return carry

    lax.fori_loop(0, out_ref.shape[0], clear, 0, unroll=4)
    first, last = plan_ref[begin], plan_ref[end]

    def step(g, carry, size, first):
        results, targets = [], []
        for u in range(size):
            s = first + g * size + u
            a = a_ref[jnp.where(s < last, plan_ref[PLAN_HEAD + s], zero_slot)]
            w = w_ref[jnp.where(s < last, plan_ref[PLAN_HEAD + 2 * length + s], fields_at[0])]
            targets.append(plan_ref[PLAN_HEAD + length + s])
            high, low = w[:cells], w[cells:]
            results.append(
                jnp.dot(
                    jnp.concatenate([a, a], axis=1),
                    jnp.concatenate([high, high, low, low], axis=0),
                    preferred_element_type=F32,
                )
            )
        for u in range(size):
            out_ref[targets[u]] += results[u]
        return carry

    huge = (last - first) // (2 * GROUP)
    lax.fori_loop(0, huge, functools.partial(step, size=2 * GROUP, first=first), 0)
    first += huge * 2 * GROUP
    large = (last - first + GROUP // 2 - 1) // GROUP
    lax.fori_loop(0, large, functools.partial(step, size=GROUP, first=first), 0)
    rest_first = first + large * GROUP
    small = jnp.where(rest_first < last, 1, 0)
    lax.fori_loop(0, small, functools.partial(step, size=GROUP // 2, first=rest_first), 0)


def transfer(plan, matrix, fields, fields_at, senders, begin, end, before, out_bricks):
    cells, lights = fields[0].shape[1:]
    whole = pl.BlockSpec(memory_space=pltpu.VMEM)
    scratch = senders * 2 * cells * lights * 2
    rows = matrix.shape[0] * cells * (end - begin) // STAGES
    return pl.pallas_call(
        functools.partial(transfer_kernel, fields_at, begin, end, len(before)),
        in_specs=[pl.BlockSpec(memory_space=pltpu.SMEM)] + [whole] * (1 + len(fields) + len(before)),
        out_specs=whole,
        out_shape=jax.ShapeDtypeStruct((out_bricks, cells, lights), F32),
        scratch_shapes=[pltpu.VMEM((senders, 2 * cells, lights), BF16)],
        compiler_params=pltpu.CompilerParams(vmem_limit_bytes=SMALL + scratch),
        cost_estimate=pl.CostEstimate(flops=0, bytes_accessed=0, transcendentals=0),
        name="transfer",
    )(pltpu.with_memory_space_constraint(plan, pltpu.SMEM), matrix, *fields, *before)


def keep_kernel(value_ref, out_ref, sem):
    copy = pltpu.make_async_copy(value_ref, out_ref, sem)
    copy.start()
    copy.wait()


def in_scalar_memory(value):
    return pl.pallas_call(
        keep_kernel,
        in_specs=[pl.BlockSpec(memory_space=pltpu.VMEM)],
        out_specs=pl.BlockSpec(memory_space=pltpu.SMEM),
        out_shape=pltpu.SMEM(value.shape, value.dtype),
        scratch_shapes=[pltpu.SemaphoreType.DMA],
        compiler_params=pltpu.CompilerParams(vmem_limit_bytes=SMALL),
        name="keep",
    )(value)


def first_of_line():
    me, n = lax.axis_index("col"), lax.axis_size("col")
    return jnp.where(me & 1 == 0, me == 0, me == n - 1)


def small_call(kernel, out_bricks, name, *args, after=()):
    whole, anywhere = pl.BlockSpec(memory_space=pltpu.VMEM), pl.BlockSpec(memory_space=pl.ANY)
    shape = args[0].shape[1:]
    return pl.pallas_call(
        kernel,
        in_specs=[whole] * len(args) + [anywhere] * len(after),
        out_specs=[whole] * len(out_bricks),
        out_shape=[jax.ShapeDtypeStruct((n, *shape), F32) for n in out_bricks],
        compiler_params=pltpu.CompilerParams(vmem_limit_bytes=SMALL),
        cost_estimate=pl.CostEstimate(flops=0, bytes_accessed=0, transcendentals=0),
        name=name,
    )(*args, *after)


def carry_kernel(mine, other, sums_ref, got_ref, *rest):
    came_refs, out_ref = rest[:-1], rest[-1]
    first = first_of_line()
    for c in range(out_ref.shape[0]):
        total = sums_ref[mine + c] + got_ref[other + c]
        if came_refs:
            total += jnp.where(first, 0.0, came_refs[0][c])
        out_ref[c] = total


def finish_kernel(half_at, owns, skipped, source_ref, sums_ref, *rest):
    out_ref = rest[-1]
    first = first_of_line()
    per = (len(rest) - 1) // len(owns)
    for h, own in enumerate(owns):
        got_ref, *ends = rest[h * per : (h + 1) * per]
        half = out_ref.shape[0] // len(owns)
        for c in range(half):
            total = source_ref[(half_at + h) * half + c] + (sums_ref[own + c] + got_ref[own - skipped + half + c])
            if ends:
                total += jnp.where(first, 0.0, ends[0][c]) + ends[1][c]
            out_ref[h * half + c] = total


def cross_kernel(came_ref, *rest):
    out_ref = rest[-1]
    half, first = out_ref.shape[0], first_of_line()
    for c in range(half):
        out_ref[c] = jnp.where(first, 0.0, came_ref[half + c])


def cut_kernel(at, value_ref, *rest):
    out_ref = rest[-1]
    out_ref[...] = value_ref[at : at + out_ref.shape[0]]


def sums_at(h, distance, pairs, half):
    order = lax.rem(distance + pairs - 1, pairs) if pairs > 1 else distance
    size = 2 * half
    return jnp.where(order == 0, h * size, (PARTS + h * (pairs - 1) + order - 1) * size)


def make_plan(row_index, col_index, live, bricks, n_row, n_col, flips):
    pairs, half = n_col // 2, bricks // PARTS
    my_row, me = lax.axis_index("row"), lax.axis_index("col")
    my_pair, my_side = me >> 1, me & 1
    column, brick = lax.div(row_index, bricks), lax.rem(row_index, bricks)
    pair, side = column >> 1, column & 1
    ahead = lax.rem(jnp.where(my_side == 0, pair - my_pair, my_pair - pair) + pairs, pairs)
    carrier = jnp.where(pair > my_pair, 0, jnp.where(pair < my_pair, 1, my_side))
    place = sums_at(lax.div(brick, half), ahead, pairs, half) + (side ^ carrier) * half + lax.rem(brick, half)

    from_row, from_brick = lax.div(col_index, bricks), lax.rem(col_index, bricks)
    turn = from_row ^ my_row if flips else lax.rem(from_row - my_row + n_row, n_row)
    sender = turn * bricks + from_brick

    n = row_index.shape[0]
    slots = jnp.arange(n, dtype=jnp.int32)
    part = jnp.where(turn == 0, 0, jnp.where(turn < n_row - 1, 1, jnp.where(place < PARTS * 2 * half, 2, 3)))
    part = jnp.where(slots < live, part, STAGES)
    key = part * n + slots
    rank = jnp.sum(key[None, :] < key[:, None], axis=1, dtype=jnp.int32)
    chosen = rank[None, :] == jnp.arange(n + GROUP, dtype=jnp.int32)[:, None]

    def in_order(value):
        return jnp.sum(jnp.where(chosen, value[None, :], 0), axis=1, dtype=jnp.int32)

    bounds = jnp.arange(PLAN_HEAD, dtype=jnp.int32)
    starts = jnp.sum(part[None, :] < bounds[:, None], axis=1, dtype=jnp.int32)
    return jnp.concatenate([starts, in_order(slots), in_order(place), in_order(sender)])


def body(source, blocks, row_index, col_index, live_count):
    bricks = source.shape[0]
    n_row, n_col = lax.axis_size("row"), lax.axis_size("col")
    pairs, half = n_col // 2, bricks // PARTS
    block = 2 * half
    flips = n_row & (n_row - 1) == 0

    swap = [(i, i ^ 1) for i in range(n_col)]
    ring = [(i, (i + 2 if i + 2 < n_col else n_col - 1) if i % 2 == 0 else (i - 2 if i > 2 else 0)) for i in range(n_col)]

    squares = [(i, (i ^ 2) if (i // 2 + i) % 2 == 0 else i ^ 1) for i in range(n_col)] if pairs % 2 == 0 else ring

    def from_turn(value, k):
        return lax.ppermute(value, "row", [(i ^ k if flips else (i + k) % n_row, i) for i in range(n_row)])

    def gather(values, direct):
        return [[from_turn(v, k) for v in values] for k in range(1, n_row if direct else n_row - 1)]

    def cut(value, at, size, after):
        return small_call(functools.partial(cut_kernel, at), (size,), "cut", value, after=after)[0]

    def forward(value, k, *after):
        return from_turn(cut(value, 0, value.shape[0], after), k)

    def apply(turns, first, end, *before):
        fields = [f for pieces in turns.values() for f in pieces]
        at = [k * bricks + sum(f.shape[0] for f in pieces[:i]) for k, pieces in turns.items() for i in range(len(pieces))]
        return transfer(plan, matrix, fields, at, n_row * bricks, first, end, before, bricks * n_col)

    leading = PARTS * block

    def at(h, distance):
        order = (distance + pairs - 1) % pairs
        return h * block if order == 0 else leading + (h * (pairs - 1) + order - 1) * block

    def scatter(lead, sums):
        if pairs == 1:
            return [[lax.ppermute(lead[:leading], "col", swap)]] * PARTS
        few = leading // LEADS
        first = [lax.ppermute(lead[i * few : (i + 1) * few], "col", swap) for i in range(LEADS)]
        far = pairs - 1
        totals = []
        for h in range(PARTS):
            kernel = functools.partial(carry_kernel, at(h, far), h * block % few)
            totals += small_call(kernel, (block,), "carry", sums, first[h * block // few])
        rest = lax.ppermute(cut(sums, leading, sums.shape[0] - leading, totals), "col", swap)
        parts = []
        for h in range(PARTS):
            came = lax.ppermute(totals[h], "col", squares)
            for distance in range(far - 1, 0, -1):
                kernel = functools.partial(carry_kernel, at(h, distance), at(h, pairs - distance) - leading)
                total = small_call(kernel, (block,), "carry", sums, rest, came)[0]
                came = lax.ppermute(total, "col", ring)
            parts.append([rest, came])
        return parts

    def finish(sums, parts, half_at, after=()):
        args = []
        for rest, *came in parts:
            args += [rest, *came]
            if came:
                crossing = small_call(cross_kernel, (half,), "cross", *came, after=after)[0]
                args.append(lax.ppermute(crossing, "col", swap))
        owns = [at(half_at + h, 0) for h in range(len(parts))]
        kernel = functools.partial(finish_kernel, half_at, owns, leading if pairs > 1 else 0)
        return small_call(kernel, (len(parts) * half,), "finish", source, sums, *args)[0]

    plan = in_scalar_memory(make_plan(row_index, col_index, live_count[0], bricks, n_row, n_col, flips))
    matrix = prepare(blocks)

    def by_row(field):
        return dict(enumerate([field, *gather(field, True)]))

    def last_row(last, sums):
        lead = apply({3: last}, 2, 3, sums)
        return lead, apply({3: last}, 3, STAGES, lead)

    if n_row == 4:
        one, two = gather([source], False)
        last = [forward(one[0][: bricks // 2], 2, matrix), forward(two[0][bricks // 2 :], 1, matrix)]
        lead, sums = last_row(last, apply({0: [source], 1: one, 2: two}, 0, 2))
    else:
        lead = sums = apply(by_row([source]), 0, STAGES)
    for _ in range(ITERS - 1):
        field = []
        parts = scatter(lead, sums)
        for begin, end in GROUPS:
            field.append(finish(sums, parts[begin:end], begin, field))
        if n_row == 4:
            one, two = gather(field, False)
            sums = apply({0: field}, 0, 1)
            last = [forward(one[0], 2), forward(two[1], 1, sums)]
            lead, sums = last_row(last, apply({1: one, 2: two}, 1, 2, sums))
        else:
            lead = sums = apply(by_row(field), 0, STAGES)
    return finish(sums, scatter(lead, sums), 0)


def solution(mesh):
    in_specs = (
        P(("row", "col"), None, None),
        P(("row", "col"), None, None),
        P(("row", "col")),
        P(("row", "col")),
        P(("row", "col")),
    )
    out_specs = P(("row", "col"), None, None)
    return jax.shard_map(body, mesh=mesh, in_specs=in_specs, out_specs=out_specs, check_vma=False)
```
